128 devices in a mesh: dp: 8 (over z_hi, x), tensor: 16 (over y, z_lo, core).
Axes of the slice: x: 4, y: 4, z: 4 (z_hi: 2, z_lo: 2; z = z_hi * 2 + z_lo), core: 2. Of those that a mesh axis runs over, the one named last changes fastest.
Arguments:
- picture_embeds: bfloat16 [1024, 6144], P(('dp', 'tensor')), may hold values from -6 to 6
- caption_embeds: bfloat16 [1024, 6144], P(('dp', 'tensor')), may hold values from -6 to 6
- picture_match_ids: int32 [1024], replicated, may hold values from 0 to 511
- caption_match_ids: int32 [1024], replicated, may hold values from 0 to 511
- logit_multiplier: float32 [1], replicated, may hold values from 10 to 40
- logit_offset: float32 [1], replicated, may hold values from -4 to -1
- branch_entries: bfloat16 [16384, 6144], P(('dp', 'tensor')), may hold values from -64 to 64, as said below
- rescale_factor: float32 [6144], replicated, may hold values from 0.1 to 1.9
- entry_projection_matrix: bfloat16 [6144, 12288], P(None, 'tensor'), may hold values from -0.078125 to 0.078125
- exit_projection_matrix: bfloat16 [12288, 6144], P('tensor'), may hold values from -0.0546875 to 0.0546875
Outputs:
- image_grad: float32 [1024, 6144], P(('dp', 'tensor'))
- token_grad: float32 [16384, 6144], P(('dp', 'tensor'))
The draws below stay inside these ranges and needn't reach their ends.
Inputs may be any that keep to these rules, and one draw needn't show every extreme that they name: `branch_entries`: token rows.
All inputs are finite; a program needn't handle non-finite values.
Results may differ from the reference program's by a relative error of at most 0.0047.
Values may be sent and summed in bfloat16 or wider, within the bound.
A program may use at most 192 MiB of HBM per device.

```python
import math
import jax
import jax.numpy as jnp
from jax import lax

D = 6144
FF = 12288
PATCHES = 256
IMG_MB = 8
GROUP_IMG = 128
BATCH = 1024
TOK_ALL = 16384
N_DP = 8


def draw_picture_embeds(key, part):
    key = jax.random.fold_in(key, 11)
    key_values, key_scale = jax.random.split(key)
    values = jnp.clip(jax.random.normal(key_values, (BATCH, D), jnp.float32), -6.0, 6.0)
    scale = jnp.exp(jax.random.uniform(key_scale, (BATCH, 1), jnp.float32, 0.0, math.log(10.0)))
    return jnp.clip(values * scale * D ** (-0.5), -6.0, 6.0).astype(jnp.bfloat16)


def draw_caption_embeds(key, part):
    key = jax.random.fold_in(key, 12)
    key_values, key_scale = jax.random.split(key)
    values = jnp.clip(jax.random.normal(key_values, (BATCH, D), jnp.float32), -6.0, 6.0)
    scale = jnp.exp(jax.random.uniform(key_scale, (BATCH, 1), jnp.float32, 0.0, math.log(10.0)))
    return jnp.clip(values * scale * D ** (-0.5), -6.0, 6.0).astype(jnp.bfloat16)


def draw_branch_entries(key, part):
    key = jax.random.fold_in(key, 13)
    key_values, key_scale = jax.random.split(key, 2)
    values = jnp.clip(jax.random.normal(key_values, (TOK_ALL, D), jnp.float32), -6.0, 6.0)
    scale = jnp.exp(jax.random.uniform(key_scale, (TOK_ALL, 1), jnp.float32, 0.0, math.log(10.0)))
    return jnp.clip(values * scale, -64.0, 64.0).astype(jnp.bfloat16)


def place_ends(entries, stream_key, least, high):
    longest = entries.shape.index(max(entries.shape))
    spots = []
    for shift in (0, 1):
        where = [jax.random.randint(jax.random.fold_in(stream_key, axis), (), 0, length) for axis, length in enumerate(entries.shape)]
        where[longest] = (where[longest] + shift) % entries.shape[longest]
        spots.append(tuple(where))
    return entries.at[spots[0]].set(least).at[spots[1]].set(high)


def level_of(rng, shape, cuts, least, high):
    def one(position, blocks):
        draws = jax.random.uniform(jax.random.fold_in(jax.random.fold_in(rng, 6), position), (blocks,), jnp.float32, least / len(cuts), high / len(cuts))
        return jnp.repeat(jnp.exp(draws), shape[position] // blocks).reshape((-1,) + (1,) * (len(shape) - position - 1))

    loudness = one(*cuts[0])
    for cut in cuts[1:]:
        loudness = loudness * one(*cut)
    return loudness


def scatter_about(own_key, dims, deviation, most, pieces=(), kind=jnp.bfloat16):
    level = level_of(own_key, dims, pieces, -0.22, 0.18) if pieces else 1.0
    values = jax.random.normal(own_key, dims, jnp.float32) * deviation * level
    return jnp.minimum(jnp.maximum(values, -most), most).astype(kind)


def setup_inputs(seed: int = 0) -> dict:
    key_of = jax.random.split(jax.random.key(seed), 11)
    picture_embeds = draw_picture_embeds(jax.random.fold_in(key_of[10], 71), 0)
    caption_embeds = draw_caption_embeds(jax.random.fold_in(key_of[10], 71), 0)
    picture_match_ids = place_ends(jax.random.randint(key_of[2], (BATCH,), 0, BATCH // 2), jax.random.fold_in(key_of[2], 1), 0, (BATCH // 2) - 1).astype(jnp.int32)
    caption_match_ids = place_ends(jax.random.randint(key_of[3], (BATCH,), 0, BATCH // 2), jax.random.fold_in(key_of[3], 1), 0, (BATCH // 2) - 1).astype(jnp.int32)
    logit_multiplier = jnp.clip(jnp.exp(jax.random.uniform(key_of[4], (1,), jnp.float32, math.log(10.0), math.log(40.0))), 10.0, 40.0)
    logit_offset = jnp.clip(jax.random.uniform(key_of[5], (1,), jnp.float32, -4.0, -1.0), -4.0, -1.0)
    branch_entries = draw_branch_entries(jax.random.fold_in(key_of[10], 71), 0)
    rescale_factor = jnp.clip(1.0 + 0.18 * jax.random.normal(key_of[7], (D,), jnp.float32), 0.1, 1.9)
    entry_projection_matrix = scatter_about(key_of[8], (D, FF), D ** -0.5, 0.078125, ((1, 16),))
    exit_projection_matrix = scatter_about(key_of[9], (FF, D), FF ** -0.5, 0.0546875, ((0, 16),))
    return dict(picture_embeds=picture_embeds, caption_embeds=caption_embeds, picture_match_ids=picture_match_ids, caption_match_ids=caption_match_ids, logit_multiplier=logit_multiplier, logit_offset=logit_offset, branch_entries=branch_entries, rescale_factor=rescale_factor, entry_projection_matrix=entry_projection_matrix, exit_projection_matrix=exit_projection_matrix)


epsilon = 1e-06

def unit_rows(rows):
    values = rows.astype(jnp.float32)
    scale = lax.rsqrt(lax.optimization_barrier(jnp.sum(values * values, axis=-1)) + epsilon)
    return (scale, values * scale[:, None])

def layer_stats(rows):
    values = rows.astype(jnp.float32)
    centered = values - lax.optimization_barrier(jnp.mean(values, axis=-1, keepdims=True))
    inverse = lax.rsqrt(lax.optimization_barrier(jnp.mean(centered * centered, axis=-1, keepdims=True)) + epsilon)
    return (inverse, centered * inverse)

def gelu_slope(values):
    cumulative = 0.5 * (1.0 + lax.erf(values * 0.7071067811865476))
    density = jnp.exp(-0.5 * values * values) * 0.3989422804014327
    return cumulative + values * density

def unit_backward(scale, unit, grad):
    return scale[:, None] * (grad - unit * lax.optimization_barrier(jnp.sum(unit * grad, axis=-1, keepdims=True)))

def reference(picture_embeds, caption_embeds, picture_match_ids, caption_match_ids, logit_multiplier, logit_offset, branch_entries, rescale_factor, entry_projection_matrix, exit_projection_matrix):
    img_scale, img_exact = unit_rows(picture_embeds)
    picture_direction = img_exact.astype(jnp.bfloat16)
    _, txt_exact = unit_rows(caption_embeds)
    caption_direction = txt_exact.astype(jnp.bfloat16)
    multiplier_scalar = logit_multiplier[0]
    offset_scalar = logit_offset[0]

    def block_grad(inputs):
        normalized_directions, img_ids = inputs
        similarity_scores = multiplier_scalar * jnp.dot(normalized_directions, caption_direction.T, preferred_element_type=jnp.float32) + offset_scalar
        match_signs = jnp.where(img_ids[:, None] == caption_match_ids[None, :], 1.0, -1.0).astype(jnp.float32)
        loss_multiplier = (-match_signs * multiplier_scalar * jax.nn.sigmoid(-match_signs * similarity_scores)).astype(jnp.bfloat16)
        return jnp.dot(loss_multiplier, caption_direction, preferred_element_type=jnp.float32)
    unit_grad = lax.map(block_grad, (picture_direction.reshape(N_DP, GROUP_IMG, D), picture_match_ids.reshape(N_DP, GROUP_IMG)))
    unit_grad = unit_grad.reshape(BATCH, D)
    image_grad = unit_backward(img_scale, img_exact, unit_grad)
    cot_rows = image_grad.reshape(N_DP, GROUP_IMG, D)[:, :IMG_MB, :].reshape(N_DP * IMG_MB, D)
    inverse, normed = layer_stats(branch_entries)
    ln_in = (normed * rescale_factor).astype(jnp.bfloat16)
    pre_act = jnp.dot(ln_in, entry_projection_matrix, preferred_element_type=jnp.float32)
    hid_grad = jnp.dot(cot_rows.astype(jnp.bfloat16), exit_projection_matrix.T, preferred_element_type=jnp.float32)
    slope = gelu_slope(pre_act.reshape(N_DP * IMG_MB, PATCHES, FF))
    pre_grad = (hid_grad[:, None, :] * slope).reshape(TOK_ALL, FF).astype(jnp.bfloat16)
    ln_grad = jnp.dot(pre_grad, entry_projection_matrix.T, preferred_element_type=jnp.float32)
    scaled = ln_grad * rescale_factor
    tok_cot = jnp.repeat(cot_rows, PATCHES, axis=0)
    token_grad = tok_cot + inverse * (scaled - lax.optimization_barrier(jnp.mean(scaled, axis=-1, keepdims=True)) - normed * lax.optimization_barrier(jnp.mean(scaled * normed, axis=-1, keepdims=True)))
    return (image_grad, token_grad)
```

```python
import jax
import jax.numpy as jnp
from jax import lax
from jax.experimental import pallas as pl
from jax.experimental.pallas import tpu as pltpu
from jax.sharding import PartitionSpec as P

EPS = 1e-06
MESH = pl.DeviceIdType.MESH
F32 = jnp.float32
BF16 = jnp.bfloat16
D = 6144
HALF = D // 2
HB = 768
ROWS = 128
CH = 512
N = D // CH
AHEAD = 3


def gelu_slope(values):
    cumulative = 0.5 * (1.0 + lax.erf(values * 0.7071067811865476))
    density = jnp.exp(-0.5 * values * values) * 0.3989422804014327
    return cumulative + values * density


def dot_nt(left, right):
    return lax.dot_general(left, right, (((1,), (1,)), ((), ())), preferred_element_type=F32)


def kernel(
    pic_ref, cap_ref, img_ids, txt_ids, mult_ref, offs_ref, tok_ref, gain_ref, w1, wx_hbm,
    img_out, tok_out, w3,
    ln, wbuf, pre, grad, m1o, m2o, m1i, m2i, text, wx, stack, unit, fold, fold_in, tx, exact, cot, cotf, hid, stat,
    s_send, s_tok, s_fwd, s_z, s_x, s_own, s_for, s_m1, s_m2, s_small, s_hid, s_w, s_wx,
):
    d = lax.axis_index("dp")
    t = lax.axis_index("tensor")
    x, zh = d % 4, d // 4
    y, zl, c = t // 4, (t // 2) % 2, t % 2
    z = 2 * zh + zl

    def dev(x_, y_, z_, c_):
        return ((z_ // 2) * 4 + x_, y_ * 4 + (z_ % 2) * 2 + c_)

    yp, ym = dev(x, (y + 1) % 4, z, c), dev(x, (y + 3) % 4, z, c)
    zp, zm = dev(x, y, (z + 1) % 4, c), dev(x, y, (z + 3) % 4, c)
    xp, xm = dev((x + 1) % 4, y, z, c), dev((x + 3) % 4, y, z, c)
    mate = (d, y * 4 + zl * 2 + (1 - c))

    def send(src, dst, ssem, rsem, device):
        pltpu.make_async_remote_copy(
            src_ref=src, dst_ref=dst, send_sem=ssem, recv_sem=rsem, device_id=device, device_id_type=MESH
        ).start()

    def wait(ref, sem):
        pltpu.make_async_copy(ref, ref, sem).wait()

    slot = d * 2 + zl

    def text_peer(s):
        other = (slot + s) % 16
        return (other // 2, y * 4 + (other % 2) * 2 + c)

    bar = pltpu.get_barrier_semaphore()

    def greet(s, _):
        pl.semaphore_signal(bar, 1, device_id=text_peer(s), device_id_type=MESH)
        pl.semaphore_signal(bar, 1, device_id=(d, (t + s) % 16), device_id_type=MESH)
        return 0

    lax.fori_loop(1, 16, greet, 0)

    pltpu.make_async_copy(wx_hbm, wx, s_wx).start()

    img = pic_ref[...].astype(F32)
    img_scale = lax.rsqrt(jnp.sum(img * img, axis=-1, keepdims=True) + EPS)
    img_exact = img * img_scale
    exact[...] = img_exact
    stat[2, 0:8] = jnp.broadcast_to(img_scale, (8, 128))
    stack[y] = jnp.concatenate([img_exact[:, :HALF], img_exact[:, HALF:]], axis=0).astype(BF16)
    cap = cap_ref[...].astype(F32)
    tx[c] = cap * lax.rsqrt(jnp.sum(cap * cap, axis=-1, keepdims=True) + EPS)

    def norm_rows(i, _):
        rows = pl.ds(pl.multiple_of(i * 16, 16), 16)
        values = tok_ref[rows, :].astype(F32)
        mean = jnp.mean(values, axis=-1, keepdims=True)
        centered = values - mean
        inverse = lax.rsqrt(jnp.mean(centered * centered, axis=-1, keepdims=True) + EPS)
        stat[0, rows] = jnp.broadcast_to(mean, (16, 128))
        stat[1, rows] = jnp.broadcast_to(inverse, (16, 128))
        out = (centered * inverse * gain_ref[...]).astype(BF16)
        for k in range(N):
            ln[k, rows, :] = out[:, k * CH:(k + 1) * CH]
        return 0

    lax.fori_loop(0, ROWS // 16, norm_rows, 0)

    pl.semaphore_wait(bar, 30)

    send(tx.at[c], tx.at[c], s_small.at[0], s_small.at[1], mate)

    def send_images(r, _):
        send(stack.at[y], stack.at[y], s_small.at[2], s_small.at[3], dev(x, (y + r) % 4, z, c))
        return 0

    lax.fori_loop(1, 4, send_images, 0)

    xpar = x % 2

    def piece(k, par, p):
        return pl.ds(pl.multiple_of(k * CH + par * 256 + p * 128, 128), 128)

    def chunk(k):
        return pl.ds(pl.multiple_of(k * CH, CH), CH)

    def send_own(k):
        send(ln.at[k, pl.ds(0, 128)], ln.at[k, pl.ds(384, 128)], s_send.at[0], s_tok.at[0, k], yp)
        send(ln.at[k, pl.ds(0, 128)], ln.at[k, pl.ds(128, 128)], s_send.at[1], s_tok.at[1, k], ym)
        send(w1.at[piece(k, xpar, 0)], w3.at[1, piece(k, xpar, 0)], s_send.at[2], s_z.at[0, k], zm)
        send(w1.at[piece(k, xpar, 1)], w3.at[1, piece(k, xpar, 1)], s_send.at[3], s_z.at[1, k], zp)
        send(w1.at[chunk(k)], w3.at[0, chunk(k)], s_send.at[4], s_own.at[k], mate)

    def first(k, _):
        send_own(k)
        return 0

    lax.fori_loop(0, AHEAD, first, 0)

    wait(tx.at[0], s_small.at[1])
    both = jnp.concatenate([tx[0], tx[1]], axis=0)
    mine = jnp.where(c == 0, both[:, :HALF], both[:, HALF:]).astype(BF16)
    text_rows = pl.ds(pl.multiple_of(slot * 16, 16), 16)
    text_cols = pl.ds(pl.multiple_of(c * HALF, HALF), HALF)
    text[text_rows, text_cols] = mine

    def send_texts(s, _):
        part = text.at[text_rows, text_cols]
        send(part, part, s_small.at[4], s_small.at[5], text_peer(s))
        return 0

    lax.fori_loop(1, 16, send_texts, 0)
    pre[...] = jnp.zeros_like(pre)

    def load(k, b):
        pltpu.make_async_copy(w1.at[chunk(k)], wbuf.at[b, :, pl.ds(0, HB)], s_w.at[b]).start()
        for j in range(3):
            pltpu.make_async_copy(w3.at[j, chunk(k)], wbuf.at[b, :, pl.ds((j + 1) * HB, HB)], s_w.at[b]).start()

    def gather_step(k, _):
        @pl.when(k < N)
        def _():
            wait(ln.at[0, pl.ds(0, 128)], s_tok.at[0, k])
            wait(ln.at[0, pl.ds(0, 128)], s_tok.at[1, k])
            send(ln.at[k, pl.ds(384, 64)], ln.at[k, pl.ds(256, 64)], s_send.at[5], s_fwd.at[0, k], yp)
            send(ln.at[k, pl.ds(192, 64)], ln.at[k, pl.ds(320, 64)], s_send.at[6], s_fwd.at[1, k], ym)
            wait(w3.at[1, pl.ds(0, 128)], s_z.at[0, k])
            wait(w3.at[1, pl.ds(0, 128)], s_z.at[1, k])
            send(w3.at[1, piece(k, xpar, 0)], w3.at[1, piece(k, xpar, 0)], s_send.at[7], s_x.at[0, k], xm)
            send(w3.at[1, piece(k, xpar, 1)], w3.at[1, piece(k, xpar, 1)], s_send.at[8], s_x.at[1, k], xp)

        @pl.when(k + AHEAD < N)
        def _():
            send_own(k + AHEAD)

        @pl.when(jnp.logical_and(k >= 1, k < N + 1))
        def _():
            q = k - 1
            wait(ln.at[0, pl.ds(0, 64)], s_fwd.at[0, q])
            wait(ln.at[0, pl.ds(0, 64)], s_fwd.at[1, q])
            wait(w3.at[1, pl.ds(0, 128)], s_x.at[0, q])
            wait(w3.at[1, pl.ds(0, 128)], s_x.at[1, q])
            send(w3.at[1, chunk(q)], w3.at[2, chunk(q)], s_send.at[9], s_for.at[q], mate)

        @pl.when(jnp.logical_and(k >= 2, k < N + 2))
        def _():
            q = k - 2
            wait(w3.at[0, pl.ds(0, CH)], s_own.at[q])
            wait(w3.at[2, pl.ds(0, CH)], s_for.at[q])
            load(q, q % 2)

        @pl.when(k >= 3)
        def _():
            q = k - 3
            b = q % 2
            wait(wbuf.at[b], s_w.at[b])

            def columns(j, _):
                cols = pl.ds(pl.multiple_of(j * HB, HB), HB)
                pre[:, cols] += jnp.dot(ln[q], wbuf[b, :, cols], preferred_element_type=F32)
                return 0

            lax.fori_loop(0, 4, columns, 0)

        @pl.when(k == 1)
        def _():
            wait(text.at[pl.ds(0, 240), pl.ds(0, HALF)], s_small.at[5])
            half = text.at[:, text_cols]
            send(half, half, s_small.at[6], s_small.at[7], mate)

        @pl.when(k == 2)
        def _():
            wait(stack.at[pl.ds(0, 3)], s_small.at[3])
            wait(text.at[:, pl.ds(0, HALF)], s_small.at[7])
            for pair in range(2):
                a = stack[2 * pair].astype(F32)
                b = stack[2 * pair + 1].astype(F32)
                unit[pair * 16:(pair + 1) * 16, :HALF] = jnp.concatenate([a[:8], b[:8]], axis=0).astype(BF16)
                unit[pair * 16:(pair + 1) * 16, HALF:] = jnp.concatenate([a[8:], b[8:]], axis=0).astype(BF16)
            multiplier = mult_ref[0]
            logits = multiplier * dot_nt(unit[...], text[...]) + offs_ref[0]
            labels = jnp.where(img_ids[...] == txt_ids[...], 1.0, -1.0).astype(F32)
            coef = (-labels * multiplier * jax.nn.sigmoid(-labels * logits)).astype(BF16)

            def fold_cols(j, _):
                cols = pl.ds(pl.multiple_of(j * 1024, 1024), 1024)
                part = jnp.dot(coef, text[:, cols], preferred_element_type=F32)
                for i in range(4):
                    fold[i, :, cols] = part[i * 8:(i + 1) * 8]
                return 0

            lax.fori_loop(0, 6, fold_cols, 0)

            def send_sums(r, _):
                other = (y + r) % 4
                send(fold.at[other], fold_in.at[r - 1], s_small.at[8], s_small.at[9], dev(x, other, z, c))
                return 0

            lax.fori_loop(1, 4, send_sums, 0)

        @pl.when(k == 4)
        def _():
            wait(fold_in, s_small.at[9])
            total = fold[y] + fold_in[0] + fold_in[1] + fold_in[2]
            ex = exact[...]
            scale = stat[2, 0:8, 0:1]
            g = scale * (total - ex * jnp.sum(ex * total, axis=-1, keepdims=True))
            img_out[...] = g

            @pl.when(t == 0)
            def _():
                cot[...] = jnp.concatenate([g[:, :HALF], g[:, HALF:]], axis=0).astype(BF16)

                def send_cot(s, _):
                    send(cot, cot, s_small.at[10], s_small.at[11], (d, s))
                    return 0

                lax.fori_loop(1, 16, send_cot, 0)

        @pl.when(k == 6)
        def _():
            @pl.when(t != 0)
            def _():
                wait(cot, s_small.at[11])

            cotf[...] = cot[...].astype(F32)
            wait(wx, s_wx)
            for j in range(3):
                low = dot_nt(cot[...], wx[j * 256:(j + 1) * 256, :HALF])
                high = dot_nt(cot[...], wx[j * 256:(j + 1) * 256, HALF:])
                hid[0, :, j * 256:(j + 1) * 256] = low[:8] + high[8:]
            send(hid.at[0], hid.at[1], s_small.at[12], s_hid.at[0], mate)
            send(hid.at[0], hid.at[2], s_small.at[13], s_hid.at[1], (d, y * 4 + (1 - zl) * 2 + c))
            send(hid.at[0], hid.at[3], s_small.at[14], s_hid.at[2], (d, y * 4 + (1 - zl) * 2 + (1 - c)))

        return 0

    lax.fori_loop(0, N + 3, gather_step, 0)
    load(0, 0)
    for j in range(3):
        wait(hid.at[0], s_hid.at[j])

    def slope_block(i, _):
        r, j = i // 4, i % 4
        rows = pl.ds(pl.multiple_of(r * ROWS, ROWS), ROWS)
        cols = pl.ds(pl.multiple_of(j * HB, HB), HB)
        image = ((y + r) % 4) * 2 + zl
        factor = hid[j, pl.ds(image, 1), :]
        grad[rows, cols] = (factor * gelu_slope(pre[rows, cols])).astype(BF16)
        return 0

    lax.fori_loop(0, 16, slope_block, 0)

    def pend(n, side):
        return (
            pl.ds(pl.multiple_of((n // 6) * 128 + side * 64, 64), 64),
            pl.ds(pl.multiple_of((n % 6) * CH, CH), CH),
        )

    def kept(n):
        return (
            pl.ds(pl.multiple_of(256 + (n // 6) * 128, 128), 128),
            pl.ds(pl.multiple_of((n % 6) * CH, CH), CH),
        )

    def scatter_step(n, carry):
        @pl.when(n + 1 < N)
        def _():
            load(n + 1, (n + 1) % 2)

        @pl.when(n < N)
        def _():
            b = n % 2
            wait(wbuf.at[b], s_w.at[b])
            part = dot_nt(grad[...], wbuf[b])
            m1o[n, 0] = part[256:320].astype(BF16)
            m1o[n, 1] = part[320:384].astype(BF16)
            send(m1o.at[n, 0], m1i.at[n, 0], s_send.at[10], s_m1.at[0, n], yp)
            send(m1o.at[n, 1], m1i.at[n, 1], s_send.at[11], s_m1.at[1, n], ym)
            pre[pend(n, 0)] = part[128:192]
            m2o[n, 0, 64:128] = part[192:256].astype(BF16)
            m2o[n, 1, 0:64] = part[384:448].astype(BF16)
            pre[pend(n, 1)] = part[448:512]
            pre[kept(n)] = part[0:128]

        @pl.when(jnp.logical_and(n >= 2, n < N + 2))
        def _():
            q = n - 2
            wait(m1i.at[0, 0], s_m1.at[0, q])
            m2o[q, 0, 0:64] = (pre[pend(q, 0)] + m1i[q, 0].astype(F32)).astype(BF16)
            send(m2o.at[q, 0], m2i.at[q, 0], s_send.at[12], s_m2.at[0, q], yp)
            wait(m1i.at[0, 0], s_m1.at[1, q])
            m2o[q, 1, 64:128] = (pre[pend(q, 1)] + m1i[q, 1].astype(F32)).astype(BF16)
            send(m2o.at[q, 1], m2i.at[q, 1], s_send.at[13], s_m2.at[1, q], ym)

        @pl.when(n >= 5)
        def _():
            q = n - 5
            wait(m2i.at[0, 0], s_m2.at[0, q])
            wait(m2i.at[0, 0], s_m2.at[1, q])
            cols = chunk(q)
            total = pre[kept(q)] + m2i[q, 0].astype(F32) + m2i[q, 1].astype(F32)
            e = total * gain_ref[:, cols]
            normed = (tok_ref[:, cols].astype(F32) - stat[0, :, 0:1]) * stat[1, :, 0:1]
            pre[kept(q)] = e
            stat[3] += jnp.broadcast_to(jnp.sum(e, axis=-1, keepdims=True), (128, 128))
            stat[4] += jnp.broadcast_to(jnp.sum(e * normed, axis=-1, keepdims=True), (128, 128))

        return carry

    stat[3] = jnp.zeros((128, 128), F32)
    stat[4] = jnp.zeros((128, 128), F32)
    lax.fori_loop(0, N + 5, scatter_step, 0)

    own_image = t // 2

    def finish(q, _):
        cols = chunk(q)
        inverse = stat[1, :, 0:1]
        normed = (tok_ref[:, cols].astype(F32) - stat[0, :, 0:1]) * inverse
        cot_cols = pl.ds(pl.multiple_of((q % 6) * CH, CH), CH)
        row = cotf[pl.ds((q // 6) * 8 + own_image, 1), cot_cols]
        tok_out[:, cols] = row + inverse * (
            pre[kept(q)] - stat[3, :, 0:1] * (1.0 / D) - normed * (stat[4, :, 0:1] * (1.0 / D))
        )
        return 0

    lax.fori_loop(0, N, finish, 0)

    wait(tx.at[0], s_small.at[0])
    wait(stack.at[pl.ds(0, 3)], s_small.at[2])
    wait(text.at[pl.ds(0, 240), pl.ds(0, HALF)], s_small.at[4])
    wait(text.at[:, pl.ds(0, HALF)], s_small.at[6])
    wait(fold_in, s_small.at[8])

    @pl.when(t == 0)
    def _():
        for _i in range(15):
            wait(cot, s_small.at[10])

    for j in range(3):
        wait(hid.at[0], s_small.at[12 + j])
    for j in range(2):
        wait(ln.at[:, pl.ds(0, 128)], s_send.at[j])
        wait(w1.at[pl.ds(0, N * 128)], s_send.at[2 + j])
        wait(ln.at[:, pl.ds(0, 64)], s_send.at[5 + j])
        wait(w1.at[pl.ds(0, N * 128)], s_send.at[7 + j])
        wait(m1o.at[:, 0], s_send.at[10 + j])
        wait(m2o.at[:, 0], s_send.at[12 + j])
    wait(w1, s_send.at[4])
    wait(w1, s_send.at[9])


def body(
    picture_embeds, caption_embeds, picture_match_ids, caption_match_ids, logit_multiplier, logit_offset,
    branch_entries, rescale_factor, entry_projection_matrix, exit_projection_matrix,
):
    d = lax.axis_index("dp")
    t = lax.axis_index("tensor")
    img_ids = picture_match_ids.reshape(8, 4, 4, 8)
    img_ids = lax.dynamic_slice(img_ids, (d, 0, t % 4, 0), (1, 4, 1, 8)).reshape(32, 1)
    txt_ids = caption_match_ids.reshape(8, 4, 4, 8)
    txt_ids = lax.dynamic_slice(txt_ids, (0, t // 4, 0, 0), (8, 1, 4, 8)).reshape(1, 256)
    vmem = pl.BlockSpec(memory_space=pltpu.VMEM)
    smem = pl.BlockSpec(memory_space=pltpu.SMEM)
    anyw = pl.BlockSpec(memory_space=pl.ANY)
    dma = pltpu.SemaphoreType.DMA
    image_grad, token_grad, _ = pl.pallas_call(
        kernel,
        out_shape=(
            jax.ShapeDtypeStruct((8, D), F32),
            jax.ShapeDtypeStruct((ROWS, D), F32),
            jax.ShapeDtypeStruct((3, D, HB), BF16),
        ),
        in_specs=[vmem, vmem, vmem, vmem, smem, smem, vmem, vmem, anyw, anyw],
        out_specs=(vmem, vmem, anyw),
        scratch_shapes=[
            pltpu.VMEM((N, 4 * ROWS, CH), BF16),
            pltpu.VMEM((2, CH, 4 * HB), BF16),
            pltpu.VMEM((4 * ROWS, 4 * HB), F32),
            pltpu.VMEM((4 * ROWS, 4 * HB), BF16),
            pltpu.VMEM((N, 2, 64, CH), BF16),
            pltpu.VMEM((N, 2, 128, CH), BF16),
            pltpu.VMEM((N, 2, 64, CH), BF16),
            pltpu.VMEM((N, 2, 128, CH), BF16),
            pltpu.VMEM((256, D), BF16),
            pltpu.VMEM((HB, D), BF16),
            pltpu.VMEM((4, 16, HALF), BF16),
            pltpu.VMEM((32, D), BF16),
            pltpu.VMEM((4, 8, D), F32),
            pltpu.VMEM((3, 8, D), F32),
            pltpu.VMEM((2, 8, D), F32),
            pltpu.VMEM((8, D), F32),
            pltpu.VMEM((16, HALF), BF16),
            pltpu.VMEM((16, HALF), F32),
            pltpu.VMEM((4, 8, HB), F32),
            pltpu.VMEM((5, 128, 128), F32),
            dma((14,)),
            dma((2, N)),
            dma((2, N)),
            dma((2, N)),
            dma((2, N)),
            dma((N,)),
            dma((N,)),
            dma((2, N)),
            dma((2, N)),
            dma((15,)),
            dma((3,)),
            dma((2,)),
            dma(()),
        ],
        compiler_params=pltpu.CompilerParams(
            collective_id=0, has_side_effects=True, vmem_limit_bytes=62 * 2**20
        ),
    )(
        picture_embeds, caption_embeds, img_ids, txt_ids, logit_multiplier, logit_offset,
        branch_entries, rescale_factor.reshape(1, D), entry_projection_matrix, exit_projection_matrix,
    )
    return (image_grad, token_grad)


def solution(mesh):
    in_specs = (
        P(("dp", "tensor"), None),
        P(("dp", "tensor"), None),
        P(),
        P(),
        P(),
        P(),
        P(("dp", "tensor"), None),
        P(),
        P(None, "tensor"),
        P("tensor", None),
    )
    out_specs = (P(("dp", "tensor"), None), P(("dp", "tensor"), None))
    return jax.shard_map(body, mesh=mesh, in_specs=in_specs, out_specs=out_specs, check_vma=False)
```

```python
import jax
import jax.numpy as jnp
from jax import lax
from jax.experimental import pallas as pl
from jax.experimental.pallas import tpu as pltpu
from jax.sharding import PartitionSpec as P

EPS = 1e-06
MESH = pl.DeviceIdType.MESH
F32 = jnp.float32
BF16 = jnp.bfloat16
D = 6144
HALF = D // 2
HB = 768
ROWS = 128
CH = 512
N = D // CH
AHEAD = 4
LAG_FWD = 2
LAG_LOAD = 4
STEP_RELAY, STEP_TEXT, STEP_LOSS, STEP_IMAGE, STEP_COT, STEP_HIDDEN = 2, 5, 6, 8, 9, 11
AHEAD_FIRST = 2
STEP_REST = 3


def gelu_slope(values):
    cumulative = 0.5 * (1.0 + lax.erf(values * 0.7071067811865476))
    density = jnp.exp(-0.5 * values * values) * 0.3989422804014327
    return cumulative + values * density


def dot_nt(left, right):
    return lax.dot_general(left, right, (((1,), (1,)), ((), ())), preferred_element_type=F32)


def kernel(
    pic_ref, cap_ref, pic_ids, cap_ids, mult_ref, offs_ref, tok_ref, gain_ref, w1, wx_hbm,
    img_out, scaled_out, stat_out, row_out, w3,
    ln, wbuf, pre, grad, m1o, m2o, m1i, m2i, text, wx, stack, unit, fold, fold_in, tx, exact, cot, cotf, hid, stat,
    s_send, s_tok, s_fwd, s_z, s_x, s_own, s_for, s_m1, s_m2, s_small, s_hid, s_w, s_wx, s_out,
):
    d = lax.axis_index("dp")
    t = lax.axis_index("tensor")
    x, zh = d % 4, d // 4
    y, zl, c = t // 4, (t // 2) % 2, t % 2
    z = 2 * zh + zl

    def dev(x_, y_, z_, c_):
        return ((z_ // 2) * 4 + x_, y_ * 4 + (z_ % 2) * 2 + c_)

    yp, ym = dev(x, (y + 1) % 4, z, c), dev(x, (y + 3) % 4, z, c)
    zp, zm = dev(x, y, (z + 1) % 4, c), dev(x, y, (z + 3) % 4, c)
    xp, xm = dev((x + 1) % 4, y, z, c), dev((x + 3) % 4, y, z, c)
    mate = (d, y * 4 + zl * 2 + (1 - c))

    def send(src, dst, ssem, rsem, device):
        pltpu.make_async_remote_copy(
            src_ref=src, dst_ref=dst, send_sem=ssem, recv_sem=rsem, device_id=device, device_id_type=MESH
        ).start()

    def wait(ref, sem):
        pltpu.make_async_copy(ref, ref, sem).wait()

    near = (d, y * 4 + (1 - zl) * 2 + c)
    near_mate = (d, y * 4 + (1 - zl) * 2 + (1 - c))
    urgent = jnp.logical_and(zl == 0, c == 0)
    early = t == 0

    bar = pltpu.get_barrier_semaphore()

    def greet(r, _):
        for peer in (dev((x + r) % 4, y, z, c), dev(x, (y + r) % 4, z, c), dev(x, y, (z + r) % 4, c)):
            pl.semaphore_signal(bar, 1, device_id=peer, device_id_type=MESH)
        return 0

    lax.fori_loop(1, 4, greet, 0)
    for peer in (mate, near_mate):
        pl.semaphore_signal(bar, 1, device_id=peer, device_id_type=MESH)

    a0, b0 = jnp.where(c == 0, x, z), jnp.where(c == 0, z, x)

    def text_device(a, b):
        return dev(jnp.where(c == 0, a, b), y, jnp.where(c == 0, b, a), c)

    def text_rows(a, b):
        x_, z_ = jnp.where(c == 0, a, b), jnp.where(c == 0, b, a)
        return pl.ds(pl.multiple_of((((z_ // 2) * 4 + x_) * 2 + z_ % 2) * 16, 16), 16)

    text_cols = pl.ds(pl.multiple_of(c * HALF, HALF), HALF)

    pltpu.make_async_copy(wx_hbm, wx, s_wx).start()

    img = pic_ref[...].astype(F32)
    img_scale = lax.rsqrt(jnp.sum(img * img, axis=-1, keepdims=True) + EPS)
    img_exact = img * img_scale
    exact[...] = img_exact
    stat[2, 0:8] = jnp.broadcast_to(img_scale, (8, 128))
    stack[y] = jnp.concatenate([img_exact[:, :HALF], img_exact[:, HALF:]], axis=0).astype(BF16)
    cap = cap_ref[...].astype(F32)
    tx[c] = cap * lax.rsqrt(jnp.sum(cap * cap, axis=-1, keepdims=True) + EPS)

    def norm_rows(i, _):
        rows = pl.ds(pl.multiple_of(i * 16, 16), 16)
        values = tok_ref[rows, :].astype(F32)
        mean = jnp.mean(values, axis=-1, keepdims=True)
        centered = values - mean
        inverse = lax.rsqrt(jnp.mean(centered * centered, axis=-1, keepdims=True) + EPS)
        stat[0, rows] = jnp.broadcast_to(mean, (16, 128))
        stat[1, rows] = jnp.broadcast_to(inverse, (16, 128))
        out = (centered * inverse * gain_ref[...]).astype(BF16)
        for k in range(N):
            ln[k, rows, :] = out[:, k * CH:(k + 1) * CH]
        return 0

    lax.fori_loop(0, ROWS // 16, norm_rows, 0)

    pl.semaphore_wait(bar, 11)

    send(tx.at[c], tx.at[c], s_small.at[0], s_small.at[1], mate)

    def send_images(r, _):
        send(stack.at[y], stack.at[y], s_small.at[2], s_small.at[3], dev(x, (y + r) % 4, z, c))
        return 0

    lax.fori_loop(1, 4, send_images, 0)

    xpar = x % 2

    def piece(k, par, p):
        return pl.ds(pl.multiple_of(k * CH + par * 256 + p * 128, 128), 128)

    def chunk(k):
        return pl.ds(pl.multiple_of(k * CH, CH), CH)

    def send_tokens(k):
        send(ln.at[k, pl.ds(0, 128)], ln.at[k, pl.ds(384, 128)], s_send.at[0], s_tok.at[0, k], yp)
        send(ln.at[k, pl.ds(0, 128)], ln.at[k, pl.ds(128, 128)], s_send.at[1], s_tok.at[1, k], ym)

    def send_weights(k):
        send(w1.at[piece(k, xpar, 0)], w3.at[1, piece(k, xpar, 0)], s_send.at[2], s_z.at[0, k], zm)
        send(w1.at[piece(k, xpar, 1)], w3.at[1, piece(k, xpar, 1)], s_send.at[3], s_z.at[1, k], zp)
        send(w1.at[chunk(k)], w3.at[0, chunk(k)], s_send.at[4], s_own.at[k], mate)

    def first(k, _):
        send_tokens(k)

        @pl.when(k < AHEAD_FIRST)
        def _():
            send_weights(k)

        return 0

    lax.fori_loop(0, AHEAD, first, 0)

    wait(tx.at[0], s_small.at[1])
    both = jnp.concatenate([tx[0], tx[1]], axis=0)
    mine = jnp.where(c == 0, both[:, :HALF], both[:, HALF:]).astype(BF16)
    own_rows = text_rows(a0, b0)
    text[own_rows, text_cols] = mine

    def send_texts(i, _):
        part = text.at[own_rows, text_cols]
        send(part, part, s_small.at[4], s_small.at[5], text_device((a0 + i) % 4, b0))
        return 0

    lax.fori_loop(1, 4, send_texts, 0)

    def second(k, _):
        send_weights(k)
        return 0

    lax.fori_loop(AHEAD_FIRST, AHEAD, second, 0)
    pre[...] = jnp.zeros_like(pre)

    def load(k, b):
        pltpu.make_async_copy(w1.at[chunk(k)], wbuf.at[b, :, pl.ds(0, HB)], s_w.at[b]).start()
        for j in range(3):
            pltpu.make_async_copy(w3.at[j, chunk(k)], wbuf.at[b, :, pl.ds((j + 1) * HB, HB)], s_w.at[b]).start()

    def ids_of_images():
        row = pltpu.roll(pic_ids[pl.ds(d, 1), :], (128 - (t % 4) * 8) % 128, 1)
        image = lax.broadcasted_iota(jnp.int32, (32, 128), 0)
        lane = lax.broadcasted_iota(jnp.int32, (32, 128), 1)
        pick = lane == (image // 8) * 32 + image % 8
        values = jnp.broadcast_to(row.astype(F32), (32, 128))
        return jnp.sum(jnp.where(pick, values, 0.0), axis=-1, keepdims=True)

    def ids_of_texts():
        lane = lax.broadcasted_iota(jnp.int32, (1, 128), 1)
        halves = []
        for h in range(2):
            out = jnp.zeros((1, 128), F32)
            for i in range(4):
                row = cap_ids[h * 4 + i:h * 4 + i + 1, :]
                row = pltpu.roll(row, (i * 32 + 128 - y * 32) % 128, 1).astype(F32)
                out = jnp.where(lane // 32 == i, row, out)
            halves.append(out)
        return jnp.concatenate(halves, axis=1)

    def send_sums(r, _):
        other = (y + r) % 4
        send(fold.at[other], fold_in.at[r - 1], s_small.at[8], s_small.at[9], dev(x, other, z, c))
        return 0

    def image_gradient():
        wait(fold_in, s_small.at[9])
        total = fold[y] + fold_in[0] + fold_in[1] + fold_in[2]
        ex = exact[...]
        scale = stat[2, 0:8, 0:1]
        g = scale * (total - ex * jnp.sum(ex * total, axis=-1, keepdims=True))
        img_out[...] = g
        return g

    def gather_step(k, _):
        @pl.when(k < N)
        def _():
            wait(ln.at[0, pl.ds(0, 128)], s_tok.at[0, k])
            wait(ln.at[0, pl.ds(0, 128)], s_tok.at[1, k])
            send(ln.at[k, pl.ds(384, 64)], ln.at[k, pl.ds(256, 64)], s_send.at[5], s_fwd.at[0, k], yp)
            send(ln.at[k, pl.ds(192, 64)], ln.at[k, pl.ds(320, 64)], s_send.at[6], s_fwd.at[1, k], ym)
            wait(w3.at[1, pl.ds(0, 128)], s_z.at[0, k])
            wait(w3.at[1, pl.ds(0, 128)], s_z.at[1, k])
            send(w3.at[1, piece(k, xpar, 0)], w3.at[1, piece(k, xpar, 0)], s_send.at[7], s_x.at[0, k], xm)
            send(w3.at[1, piece(k, xpar, 1)], w3.at[1, piece(k, xpar, 1)], s_send.at[8], s_x.at[1, k], xp)

        @pl.when(k + AHEAD < N)
        def _():
            send_tokens(k + AHEAD)
            send_weights(k + AHEAD)

        @pl.when(jnp.logical_and(k >= LAG_FWD, k < N + LAG_FWD))
        def _():
            q = k - LAG_FWD
            wait(ln.at[0, pl.ds(0, 64)], s_fwd.at[0, q])
            wait(ln.at[0, pl.ds(0, 64)], s_fwd.at[1, q])
            wait(w3.at[1, pl.ds(0, 128)], s_x.at[0, q])
            wait(w3.at[1, pl.ds(0, 128)], s_x.at[1, q])
            send(w3.at[1, chunk(q)], w3.at[2, chunk(q)], s_send.at[9], s_for.at[q], mate)

        @pl.when(jnp.logical_and(k >= LAG_LOAD, k < N + LAG_LOAD))
        def _():
            q = k - LAG_LOAD
            wait(w3.at[0, pl.ds(0, CH)], s_own.at[q])
            wait(w3.at[2, pl.ds(0, CH)], s_for.at[q])
            load(q, q % 2)

        @pl.when(k >= LAG_LOAD + 1)
        def _():
            q = k - LAG_LOAD - 1
            b = q % 2
            wait(wbuf.at[b], s_w.at[b])

            def columns(j, _):
                cols = pl.ds(pl.multiple_of(j * HB, HB), HB)
                pre[:, cols] += jnp.dot(ln[q], wbuf[b, :, cols], preferred_element_type=F32)
                return 0

            lax.fori_loop(0, 4, columns, 0)

        @pl.when(k == STEP_RELAY)
        def _():
            wait(text.at[pl.ds(0, 48), pl.ds(0, HALF)], s_small.at[5])

            def relay(i, _):
                part = text.at[text_rows((a0 + i // 3) % 4, b0), text_cols]
                send(part, part, s_small.at[15], s_small.at[16], text_device(a0, (b0 + 1 + i % 3) % 4))
                return 0

            lax.fori_loop(0, 12, relay, 0)

        @pl.when(k == STEP_TEXT)
        def _():
            wait(text.at[pl.ds(0, 192), pl.ds(0, HALF)], s_small.at[16])
            half = text.at[:, text_cols]
            send(half, half, s_small.at[6], s_small.at[7], mate)

        @pl.when(k == STEP_LOSS)
        def _():
            wait(stack.at[pl.ds(0, 3)], s_small.at[3])
            wait(text.at[:, pl.ds(0, HALF)], s_small.at[7])
            for pair in range(2):
                a = stack[2 * pair].astype(F32)
                b = stack[2 * pair + 1].astype(F32)
                unit[pair * 16:(pair + 1) * 16, :HALF] = jnp.concatenate([a[:8], b[:8]], axis=0).astype(BF16)
                unit[pair * 16:(pair + 1) * 16, HALF:] = jnp.concatenate([a[8:], b[8:]], axis=0).astype(BF16)
            multiplier = mult_ref[0]
            logits = multiplier * dot_nt(unit[...], text[...]) + offs_ref[0]
            labels = jnp.where(ids_of_images() == ids_of_texts(), 1.0, -1.0).astype(F32)
            coef = (-labels * multiplier * jax.nn.sigmoid(-labels * logits)).astype(BF16)

            def fold_cols(j, _):
                cols = pl.ds(pl.multiple_of(j * 1024, 1024), 1024)
                part = jnp.dot(coef, text[:, cols], preferred_element_type=F32)
                for i in range(4):
                    fold[i, :, cols] = part[i * 8:(i + 1) * 8]
                return 0

            lax.fori_loop(0, 6, fold_cols, 0)

            @pl.when(jnp.logical_and(urgent, y != 0))
            def _():
                send_sums(4 - y, 0)

        @pl.when(jnp.logical_and(k == STEP_IMAGE, early))
        def _():
            g = image_gradient()
            cot[...] = jnp.concatenate([g[:, :HALF], g[:, HALF:]], axis=0).astype(BF16)

            def send_cot(r, _):
                send(cot, cot, s_small.at[10], s_small.at[11], dev(x, (y + r) % 4, z, c))
                return 0

            lax.fori_loop(1, 4, send_cot, 0)

        @pl.when(jnp.logical_and(k == STEP_COT, urgent))
        def _():
            @pl.when(y != 0)
            def _():
                wait(cot, s_small.at[11])

            for peer in (near, near_mate, mate):
                send(cot, cot, s_small.at[17], s_small.at[11], peer)

        @pl.when(k == STEP_HIDDEN)
        def _():
            @pl.when(jnp.logical_not(urgent))
            def _():
                wait(cot, s_small.at[11])

            cotf[...] = cot[...].astype(F32)
            wait(wx, s_wx)
            for j in range(3):
                low = dot_nt(cot[...], wx[j * 256:(j + 1) * 256, :HALF])
                high = dot_nt(cot[...], wx[j * 256:(j + 1) * 256, HALF:])
                hid[0, :, j * 256:(j + 1) * 256] = low[:8] + high[8:]
            send(hid.at[0], hid.at[1], s_small.at[12], s_hid.at[0], mate)
            send(hid.at[0], hid.at[2], s_small.at[13], s_hid.at[1], near)
            send(hid.at[0], hid.at[3], s_small.at[14], s_hid.at[2], near_mate)

        return 0

    lax.fori_loop(0, N + LAG_LOAD + 1, gather_step, 0)
    load(0, 0)

    def send_rest(r, _):
        @pl.when(jnp.logical_not(jnp.logical_and(urgent, (y + r) % 4 == 0)))
        def _():
            send_sums(r, 0)

        return 0

    lax.fori_loop(1, 4, send_rest, 0)
    for j in range(3):
        wait(hid.at[0], s_hid.at[j])

    def slope_block(i, _):
        r, j = i // 4, i % 4
        rows = pl.ds(pl.multiple_of(r * ROWS, ROWS), ROWS)
        cols = pl.ds(pl.multiple_of(j * HB, HB), HB)
        image = ((y + r) % 4) * 2 + zl
        factor = hid[j, pl.ds(image, 1), :]
        grad[rows, cols] = (factor * gelu_slope(pre[rows, cols])).astype(BF16)
        return 0

    lax.fori_loop(0, 16, slope_block, 0)

    def pend(n, side):
        return (
            pl.ds(pl.multiple_of((n // 6) * 128 + side * 64, 64), 64),
            pl.ds(pl.multiple_of((n % 6) * CH, CH), CH),
        )

    def kept(n):
        return (
            pl.ds(pl.multiple_of(256 + (n // 6) * 128, 128), 128),
            pl.ds(pl.multiple_of((n % 6) * CH, CH), CH),
        )

    def scatter_step(n, carry):
        @pl.when(n + 1 < N)
        def _():
            load(n + 1, (n + 1) % 2)

        @pl.when(n < N)
        def _():
            b = n % 2
            wait(wbuf.at[b], s_w.at[b])
            part = dot_nt(grad[...], wbuf[b])
            m1o[n, 0] = part[256:320].astype(BF16)
            m1o[n, 1] = part[320:384].astype(BF16)
            send(m1o.at[n, 0], m1i.at[n, 0], s_send.at[10], s_m1.at[0, n], yp)
            send(m1o.at[n, 1], m1i.at[n, 1], s_send.at[11], s_m1.at[1, n], ym)
            pre[pend(n, 0)] = part[128:192]
            m2o[n, 0, 64:128] = part[192:256].astype(BF16)
            m2o[n, 1, 0:64] = part[384:448].astype(BF16)
            pre[pend(n, 1)] = part[448:512]
            pre[kept(n)] = part[0:128]

        @pl.when(jnp.logical_and(n >= 2, n < N + 2))
        def _():
            q = n - 2
            wait(m1i.at[0, 0], s_m1.at[0, q])
            m2o[q, 0, 0:64] = (pre[pend(q, 0)] + m1i[q, 0].astype(F32)).astype(BF16)
            send(m2o.at[q, 0], m2i.at[q, 0], s_send.at[12], s_m2.at[0, q], yp)
            wait(m1i.at[0, 0], s_m1.at[1, q])
            m2o[q, 1, 64:128] = (pre[pend(q, 1)] + m1i[q, 1].astype(F32)).astype(BF16)
            send(m2o.at[q, 1], m2i.at[q, 1], s_send.at[13], s_m2.at[1, q], ym)

        @pl.when(n >= 5)
        def _():
            q = n - 5
            wait(m2i.at[0, 0], s_m2.at[0, q])
            wait(m2i.at[0, 0], s_m2.at[1, q])
            cols = chunk(q)
            total = pre[kept(q)] + m2i[q, 0].astype(F32) + m2i[q, 1].astype(F32)
            e = total * gain_ref[:, cols]
            normed = (tok_ref[:, cols].astype(F32) - stat[0, :, 0:1]) * stat[1, :, 0:1]
            pre[kept(q)] = e
            pltpu.make_async_copy(pre.at[kept(q)], scaled_out.at[:, cols], s_out).start()
            stat[3] += jnp.broadcast_to(jnp.sum(e, axis=-1, keepdims=True), (128, 128))
            stat[4] += jnp.broadcast_to(jnp.sum(e * normed, axis=-1, keepdims=True), (128, 128))

        @pl.when(jnp.logical_and(n == STEP_REST, jnp.logical_not(early)))
        def _():
            image_gradient()

        return carry

    stat[3] = jnp.zeros((128, 128), F32)
    stat[4] = jnp.zeros((128, 128), F32)
    lax.fori_loop(0, N + 5, scatter_step, 0)

    own_image = t // 2
    for h in range(2):
        row_out[:, h * HALF:(h + 1) * HALF] = cotf[pl.ds(h * 8 + own_image, 1), :]
    lane = lax.broadcasted_iota(jnp.int32, (128, 128), 1)
    means = jnp.where(lane == 2, stat[3], stat[4]) * (1.0 / D)
    stat_out[...] = jnp.where(lane == 0, stat[0], jnp.where(lane == 1, stat[1], means))
    wait(scaled_out, s_out)

    wait(tx.at[0], s_small.at[0])
    wait(stack.at[pl.ds(0, 3)], s_small.at[2])
    wait(text.at[pl.ds(0, 48), pl.ds(0, HALF)], s_small.at[4])
    wait(text.at[pl.ds(0, 192), pl.ds(0, HALF)], s_small.at[15])
    wait(text.at[:, pl.ds(0, HALF)], s_small.at[6])
    wait(fold_in, s_small.at[8])

    @pl.when(early)
    def _():
        for _i in range(3):
            wait(cot, s_small.at[10])

    @pl.when(urgent)
    def _():
        for _i in range(3):
            wait(cot, s_small.at[17])

    for j in range(3):
        wait(hid.at[0], s_small.at[12 + j])
    for j in range(2):
        wait(ln.at[:, pl.ds(0, 128)], s_send.at[j])
        wait(w1.at[pl.ds(0, N * 128)], s_send.at[2 + j])
        wait(ln.at[:, pl.ds(0, 64)], s_send.at[5 + j])
        wait(w1.at[pl.ds(0, N * 128)], s_send.at[7 + j])
        wait(m1o.at[:, 0], s_send.at[10 + j])
        wait(m2o.at[:, 0], s_send.at[12 + j])
    wait(w1, s_send.at[4])
    wait(w1, s_send.at[9])


def body(
    picture_embeds, caption_embeds, picture_match_ids, caption_match_ids, logit_multiplier, logit_offset,
    branch_entries, rescale_factor, entry_projection_matrix, exit_projection_matrix,
):
    vmem = pl.BlockSpec(memory_space=pltpu.VMEM)
    smem = pl.BlockSpec(memory_space=pltpu.SMEM)
    anyw = pl.BlockSpec(memory_space=pl.ANY)
    dma = pltpu.SemaphoreType.DMA
    image_grad, scaled, stats, cot_row, _ = pl.pallas_call(
        kernel,
        out_shape=(
            jax.ShapeDtypeStruct((8, D), F32),
            jax.ShapeDtypeStruct((ROWS, D), F32),
            jax.ShapeDtypeStruct((ROWS, 128), F32),
            jax.ShapeDtypeStruct((1, D), F32),
            jax.ShapeDtypeStruct((3, D, HB), BF16),
        ),
        in_specs=[vmem, vmem, vmem, vmem, smem, smem, vmem, vmem, anyw, anyw],
        out_specs=(vmem, anyw, vmem, vmem, anyw),
        scratch_shapes=[
            pltpu.VMEM((N, 4 * ROWS, CH), BF16),
            pltpu.VMEM((2, CH, 4 * HB), BF16),
            pltpu.VMEM((4 * ROWS, 4 * HB), F32),
            pltpu.VMEM((4 * ROWS, 4 * HB), BF16),
            pltpu.VMEM((N, 2, 64, CH), BF16),
            pltpu.VMEM((N, 2, 128, CH), BF16),
            pltpu.VMEM((N, 2, 64, CH), BF16),
            pltpu.VMEM((N, 2, 128, CH), BF16),
            pltpu.VMEM((256, D), BF16),
            pltpu.VMEM((HB, D), BF16),
            pltpu.VMEM((4, 16, HALF), BF16),
            pltpu.VMEM((32, D), BF16),
            pltpu.VMEM((4, 8, D), F32),
            pltpu.VMEM((3, 8, D), F32),
            pltpu.VMEM((2, 8, D), F32),
            pltpu.VMEM((8, D), F32),
            pltpu.VMEM((16, HALF), BF16),
            pltpu.VMEM((16, HALF), F32),
            pltpu.VMEM((4, 8, HB), F32),
            pltpu.VMEM((5, 128, 128), F32),
            dma((14,)),
            dma((2, N)),
            dma((2, N)),
            dma((2, N)),
            dma((2, N)),
            dma((N,)),
            dma((N,)),
            dma((2, N)),
            dma((2, N)),
            dma((18,)),
            dma((3,)),
            dma((2,)),
            dma(()),
            dma(()),
        ],
        compiler_params=pltpu.CompilerParams(
            collective_id=0, has_side_effects=True, vmem_limit_bytes=62 * 2**20
        ),
    )(
        picture_embeds, caption_embeds, picture_match_ids.reshape(8, 128), caption_match_ids.reshape(8, 128),
        logit_multiplier, logit_offset, branch_entries, rescale_factor.reshape(1, D), entry_projection_matrix, exit_projection_matrix,
    )
    inverse = stats[:, 1:2]
    normed = (branch_entries.astype(F32) - stats[:, 0:1]) * inverse
    token_grad = cot_row + inverse * (scaled - stats[:, 2:3] - normed * stats[:, 3:4])
    return (image_grad, token_grad)


def solution(mesh):
    in_specs = (
        P(("dp", "tensor"), None),
        P(("dp", "tensor"), None),
        P(),
        P(),
        P(),
        P(),
        P(("dp", "tensor"), None),
        P(),
        P(None, "tensor"),
        P("tensor", None),
    )
    out_specs = (P(("dp", "tensor"), None), P(("dp", "tensor"), None))
    return jax.shard_map(body, mesh=mesh, in_specs=in_specs, out_specs=out_specs, check_vma=False)
```

```python
import jax
import jax.numpy as jnp
from jax import lax
from jax.experimental import pallas as pl
from jax.experimental.pallas import tpu as pltpu
from jax.sharding import PartitionSpec as P

EPS = 1e-06
MESH = pl.DeviceIdType.MESH
F32 = jnp.float32
BF16 = jnp.bfloat16
D = 6144
HALF = D // 2
HB = 768
ROWS = 128
CH = 512
N = D // CH
GC = 256
G = D // GC
AHEAD = 6
LAG_FWD = 3
LAG_LOAD = 5
STEP_RELAY, STEP_TEXT, STEP_LOSS, STEP_IMAGE, STEP_COT, STEP_HIDDEN = 4, 10, 12, 16, 18, 21
AHEAD_FIRST = 4
STEP_REST = 3


def gelu_slope(values):
    cumulative = 0.5 * (1.0 + lax.erf(values * 0.7071067811865476))
    density = jnp.exp(-0.5 * values * values) * 0.3989422804014327
    return cumulative + values * density


def dot_nt(left, right):
    return lax.dot_general(left, right, (((1,), (1,)), ((), ())), preferred_element_type=F32)


def kernel(
    pic_ref, cap_ref, pic_ids, cap_ids, mult_ref, offs_ref, tok_ref, gain_ref, w1, wx_hbm,
    img_out, scaled_out, stat_out, row_out, w3,
    ln, wbuf, pre, grad, m1o, m2o, m1i, m2i, text, wx, stack, unit, fold, fold_in, tx, exact, cot, cotf, hid, stat,
    s_send, s_tok, s_fwd, s_z, s_x, s_own, s_for, s_m1, s_m2, s_small, s_hid, s_w, s_wx, s_out,
):
    d = lax.axis_index("dp")
    t = lax.axis_index("tensor")
    x, zh = d % 4, d // 4
    y, zl, c = t // 4, (t // 2) % 2, t % 2
    z = 2 * zh + zl

    def dev(x_, y_, z_, c_):
        return ((z_ // 2) * 4 + x_, y_ * 4 + (z_ % 2) * 2 + c_)

    yp, ym = dev(x, (y + 1) % 4, z, c), dev(x, (y + 3) % 4, z, c)
    zp, zm = dev(x, y, (z + 1) % 4, c), dev(x, y, (z + 3) % 4, c)
    xp, xm = dev((x + 1) % 4, y, z, c), dev((x + 3) % 4, y, z, c)
    mate = (d, y * 4 + zl * 2 + (1 - c))

    def send(src, dst, ssem, rsem, device):
        pltpu.make_async_remote_copy(
            src_ref=src, dst_ref=dst, send_sem=ssem, recv_sem=rsem, device_id=device, device_id_type=MESH
        ).start()

    def wait(ref, sem):
        pltpu.make_async_copy(ref, ref, sem).wait()

    near = (d, y * 4 + (1 - zl) * 2 + c)
    near_mate = (d, y * 4 + (1 - zl) * 2 + (1 - c))
    urgent = jnp.logical_and(zl == 0, c == 0)
    early = t == 0

    bar = pltpu.get_barrier_semaphore()

    def greet(r, _):
        for peer in (dev((x + r) % 4, y, z, c), dev(x, (y + r) % 4, z, c), dev(x, y, (z + r) % 4, c)):
            pl.semaphore_signal(bar, 1, device_id=peer, device_id_type=MESH)
        return 0

    lax.fori_loop(1, 4, greet, 0)
    for peer in (mate, near_mate):
        pl.semaphore_signal(bar, 1, device_id=peer, device_id_type=MESH)

    a0, b0 = jnp.where(c == 0, x, z), jnp.where(c == 0, z, x)

    def text_device(a, b):
        return dev(jnp.where(c == 0, a, b), y, jnp.where(c == 0, b, a), c)

    def text_rows(a, b):
        x_, z_ = jnp.where(c == 0, a, b), jnp.where(c == 0, b, a)
        return pl.ds(pl.multiple_of((((z_ // 2) * 4 + x_) * 2 + z_ % 2) * 16, 16), 16)

    text_cols = pl.ds(pl.multiple_of(c * HALF, HALF), HALF)

    pltpu.make_async_copy(wx_hbm, wx, s_wx).start()

    img = pic_ref[...].astype(F32)
    img_scale = lax.rsqrt(jnp.sum(img * img, axis=-1, keepdims=True) + EPS)
    img_exact = img * img_scale
    exact[...] = img_exact
    stat[2, 0:8] = jnp.broadcast_to(img_scale, (8, 128))
    stack[y] = jnp.concatenate([img_exact[:, :HALF], img_exact[:, HALF:]], axis=0).astype(BF16)
    cap = cap_ref[...].astype(F32)
    tx[c] = cap * lax.rsqrt(jnp.sum(cap * cap, axis=-1, keepdims=True) + EPS)

    def norm_rows(i, _):
        rows = pl.ds(pl.multiple_of(i * 16, 16), 16)
        values = tok_ref[rows, :].astype(F32)
        mean = jnp.mean(values, axis=-1, keepdims=True)
        centered = values - mean
        inverse = lax.rsqrt(jnp.mean(centered * centered, axis=-1, keepdims=True) + EPS)
        stat[0, rows] = jnp.broadcast_to(mean, (16, 128))
        stat[1, rows] = jnp.broadcast_to(inverse, (16, 128))
        out = (centered * inverse * gain_ref[...]).astype(BF16)
        for k in range(G):
            ln[k, rows, :] = out[:, k * GC:(k + 1) * GC]
        return 0

    lax.fori_loop(0, ROWS // 16, norm_rows, 0)

    pl.semaphore_wait(bar, 11)

    send(tx.at[c], tx.at[c], s_small.at[0], s_small.at[1], mate)

    xpar = x % 2

    def piece(k, par, p):
        return pl.ds(pl.multiple_of(k * GC + par * (GC // 2) + p * (GC // 4), GC // 4), GC // 4)

    def chunk(k):
        return pl.ds(pl.multiple_of(k * CH, CH), CH)

    def part_of(k):
        return pl.ds(pl.multiple_of(k * GC, GC), GC)

    def send_tokens(k):
        send(ln.at[k, pl.ds(0, 128)], ln.at[k, pl.ds(384, 128)], s_send.at[0], s_tok.at[0, k], yp)
        send(ln.at[k, pl.ds(0, 128)], ln.at[k, pl.ds(128, 128)], s_send.at[1], s_tok.at[1, k], ym)

    def send_weights(k):
        send(w1.at[piece(k, xpar, 0)], w3.at[1, piece(k, xpar, 0)], s_send.at[2], s_z.at[0, k], zm)
        send(w1.at[piece(k, xpar, 1)], w3.at[1, piece(k, xpar, 1)], s_send.at[3], s_z.at[1, k], zp)
        send(w1.at[part_of(k)], w3.at[0, part_of(k)], s_send.at[4], s_own.at[k], mate)

    def first_weights(k, _):
        send_weights(k)
        return 0

    lax.fori_loop(0, AHEAD_FIRST, first_weights, 0)

    def first_tokens(k, _):
        send_tokens(k)
        return 0

    lax.fori_loop(0, AHEAD, first_tokens, 0)

    def send_images(r, _):
        send(stack.at[y], stack.at[y], s_small.at[2], s_small.at[3], dev(x, (y + r) % 4, z, c))
        return 0

    lax.fori_loop(1, 4, send_images, 0)

    wait(tx.at[0], s_small.at[1])
    both = jnp.concatenate([tx[0], tx[1]], axis=0)
    mine = jnp.where(c == 0, both[:, :HALF], both[:, HALF:]).astype(BF16)
    own_rows = text_rows(a0, b0)
    text[own_rows, text_cols] = mine

    def send_texts(i, _):
        part = text.at[own_rows, text_cols]
        send(part, part, s_small.at[4], s_small.at[5], text_device((a0 + i) % 4, b0))
        return 0

    lax.fori_loop(1, 4, send_texts, 0)

    def second(k, _):
        send_weights(k)
        return 0

    lax.fori_loop(AHEAD_FIRST, AHEAD, second, 0)
    pre[...] = jnp.zeros_like(pre)

    def load(k, b):
        pltpu.make_async_copy(w1.at[part_of(k)], wbuf.at[b, :, pl.ds(0, HB)], s_w.at[b]).start()
        for j in range(3):
            pltpu.make_async_copy(w3.at[j, part_of(k)], wbuf.at[b, :, pl.ds((j + 1) * HB, HB)], s_w.at[b]).start()

    def load_chunk(n):
        for h in range(2):
            load(2 * n + h, 2 * (n % 2) + h)

    def ids_of_images():
        row = pltpu.roll(pic_ids[pl.ds(d, 1), :], (128 - (t % 4) * 8) % 128, 1)
        image = lax.broadcasted_iota(jnp.int32, (32, 128), 0)
        lane = lax.broadcasted_iota(jnp.int32, (32, 128), 1)
        pick = lane == (image // 8) * 32 + image % 8
        values = jnp.broadcast_to(row.astype(F32), (32, 128))
        return jnp.sum(jnp.where(pick, values, 0.0), axis=-1, keepdims=True)

    def ids_of_texts():
        lane = lax.broadcasted_iota(jnp.int32, (1, 128), 1)
        halves = []
        for h in range(2):
            out = jnp.zeros((1, 128), F32)
            for i in range(4):
                row = cap_ids[h * 4 + i:h * 4 + i + 1, :]
                row = pltpu.roll(row, (i * 32 + 128 - y * 32) % 128, 1).astype(F32)
                out = jnp.where(lane // 32 == i, row, out)
            halves.append(out)
        return jnp.concatenate(halves, axis=1)

    def send_sums(r, _):
        other = (y + r) % 4
        send(fold.at[other], fold_in.at[r - 1], s_small.at[8], s_small.at[9], dev(x, other, z, c))
        return 0

    def send_rest(r, _):
        @pl.when(jnp.logical_not(jnp.logical_and(urgent, (y + r) % 4 == 0)))
        def _():
            send_sums(r, 0)

        return 0

    def image_gradient():
        wait(fold_in, s_small.at[9])
        total = fold[y] + fold_in[0] + fold_in[1] + fold_in[2]
        ex = exact[...]
        scale = stat[2, 0:8, 0:1]
        g = scale * (total - ex * jnp.sum(ex * total, axis=-1, keepdims=True))
        img_out[...] = g
        return g

    def gather_step(k, _):
        @pl.when(k < G)
        def _():
            wait(ln.at[0, pl.ds(0, 128)], s_tok.at[0, k])
            wait(ln.at[0, pl.ds(0, 128)], s_tok.at[1, k])
            send(ln.at[k, pl.ds(384, 64)], ln.at[k, pl.ds(256, 64)], s_send.at[5], s_fwd.at[0, k], yp)
            send(ln.at[k, pl.ds(192, 64)], ln.at[k, pl.ds(320, 64)], s_send.at[6], s_fwd.at[1, k], ym)
            wait(w3.at[1, pl.ds(0, GC // 4)], s_z.at[0, k])
            wait(w3.at[1, pl.ds(0, GC // 4)], s_z.at[1, k])
            send(w3.at[1, piece(k, xpar, 0)], w3.at[1, piece(k, xpar, 0)], s_send.at[7], s_x.at[0, k], xm)
            send(w3.at[1, piece(k, xpar, 1)], w3.at[1, piece(k, xpar, 1)], s_send.at[8], s_x.at[1, k], xp)

        @pl.when(k + AHEAD < G)
        def _():
            send_tokens(k + AHEAD)
            send_weights(k + AHEAD)

        @pl.when(jnp.logical_and(k >= LAG_FWD, k < G + LAG_FWD))
        def _():
            q = k - LAG_FWD
            wait(ln.at[0, pl.ds(0, 64)], s_fwd.at[0, q])
            wait(ln.at[0, pl.ds(0, 64)], s_fwd.at[1, q])
            wait(w3.at[1, pl.ds(0, GC // 4)], s_x.at[0, q])
            wait(w3.at[1, pl.ds(0, GC // 4)], s_x.at[1, q])
            send(w3.at[1, part_of(q)], w3.at[2, part_of(q)], s_send.at[9], s_for.at[q], mate)

        @pl.when(jnp.logical_and(k >= LAG_LOAD, k < G + LAG_LOAD))
        def _():
            q = k - LAG_LOAD
            wait(w3.at[0, pl.ds(0, GC)], s_own.at[q])
            wait(w3.at[2, pl.ds(0, GC)], s_for.at[q])
            load(q, q % 4)

        @pl.when(k >= LAG_LOAD + 1)
        def _():
            q = k - LAG_LOAD - 1
            b = q % 4
            wait(wbuf.at[b], s_w.at[b])

            def columns(j, _):
                cols = pl.ds(pl.multiple_of(j * HB, HB), HB)
                pre[:, cols] += jnp.dot(ln[q], wbuf[b, :, cols], preferred_element_type=F32)
                return 0

            lax.fori_loop(0, 4, columns, 0)

        @pl.when(k == G)
        def _():
            lax.fori_loop(1, 4, send_rest, 0)

        @pl.when(k == STEP_RELAY)
        def _():
            wait(text.at[pl.ds(0, 48), pl.ds(0, HALF)], s_small.at[5])

            def relay(i, _):
                part = text.at[text_rows((a0 + i // 3) % 4, b0), text_cols]
                send(part, part, s_small.at[15], s_small.at[16], text_device(a0, (b0 + 1 + i % 3) % 4))
                return 0

            lax.fori_loop(0, 12, relay, 0)

        @pl.when(k == STEP_TEXT)
        def _():
            wait(text.at[pl.ds(0, 192), pl.ds(0, HALF)], s_small.at[16])
            half = text.at[:, text_cols]
            send(half, half, s_small.at[6], s_small.at[7], mate)

        @pl.when(k == STEP_LOSS)
        def _():
            wait(stack.at[pl.ds(0, 3)], s_small.at[3])
            wait(text.at[:, pl.ds(0, HALF)], s_small.at[7])
            for pair in range(2):
                a = stack[2 * pair].astype(F32)
                b = stack[2 * pair + 1].astype(F32)
                unit[pair * 16:(pair + 1) * 16, :HALF] = jnp.concatenate([a[:8], b[:8]], axis=0).astype(BF16)
                unit[pair * 16:(pair + 1) * 16, HALF:] = jnp.concatenate([a[8:], b[8:]], axis=0).astype(BF16)
            multiplier = mult_ref[0]
            logits = multiplier * dot_nt(unit[...], text[...]) + offs_ref[0]
            labels = jnp.where(ids_of_images() == ids_of_texts(), 1.0, -1.0).astype(F32)
            coef = (-labels * multiplier * jax.nn.sigmoid(-labels * logits)).astype(BF16)

            def fold_cols(j, _):
                cols = pl.ds(pl.multiple_of(j * 1024, 1024), 1024)
                part = jnp.dot(coef, text[:, cols], preferred_element_type=F32)
                for i in range(4):
                    fold[i, :, cols] = part[i * 8:(i + 1) * 8]
                return 0

            lax.fori_loop(0, 6, fold_cols, 0)

            @pl.when(jnp.logical_and(urgent, y != 0))
            def _():
                send_sums(4 - y, 0)

        @pl.when(jnp.logical_and(k == STEP_IMAGE, early))
        def _():
            g = image_gradient()
            cot[...] = jnp.concatenate([g[:, :HALF], g[:, HALF:]], axis=0).astype(BF16)

            def send_cot(r, _):
                send(cot, cot, s_small.at[10], s_small.at[11], dev(x, (y + r) % 4, z, c))
                return 0

            lax.fori_loop(1, 4, send_cot, 0)

        @pl.when(jnp.logical_and(k == STEP_COT, urgent))
        def _():
            @pl.when(y != 0)
            def _():
                wait(cot, s_small.at[11])

            for peer in (near, near_mate, mate):
                send(cot, cot, s_small.at[17], s_small.at[11], peer)

        @pl.when(k == STEP_HIDDEN)
        def _():
            @pl.when(jnp.logical_not(urgent))
            def _():
                wait(cot, s_small.at[11])

            cotf[...] = cot[...].astype(F32)
            wait(wx, s_wx)
            for j in range(3):
                low = dot_nt(cot[...], wx[j * 256:(j + 1) * 256, :HALF])
                high = dot_nt(cot[...], wx[j * 256:(j + 1) * 256, HALF:])
                hid[0, :, j * 256:(j + 1) * 256] = low[:8] + high[8:]
            send(hid.at[0], hid.at[1], s_small.at[12], s_hid.at[0], mate)
            send(hid.at[0], hid.at[2], s_small.at[13], s_hid.at[1], near)
            send(hid.at[0], hid.at[3], s_small.at[14], s_hid.at[2], near_mate)

        return 0

    lax.fori_loop(0, G + LAG_LOAD + 1, gather_step, 0)
    load_chunk(0)

    for j in range(3):
        wait(hid.at[0], s_hid.at[j])

    def slope_block(i, _):
        r, j = i // 4, i % 4
        rows = pl.ds(pl.multiple_of(r * ROWS, ROWS), ROWS)
        cols = pl.ds(pl.multiple_of(j * HB, HB), HB)
        image = ((y + r) % 4) * 2 + zl
        factor = hid[j, pl.ds(image, 1), :]
        grad[rows, cols] = (factor * gelu_slope(pre[rows, cols])).astype(BF16)
        return 0

    lax.fori_loop(0, 16, slope_block, 0)

    def pend(n, side):
        return (
            pl.ds(pl.multiple_of((n // 6) * 128 + side * 64, 64), 64),
            pl.ds(pl.multiple_of((n % 6) * CH, CH), CH),
        )

    def kept(n):
        return (
            pl.ds(pl.multiple_of(256 + (n // 6) * 128, 128), 128),
            pl.ds(pl.multiple_of((n % 6) * CH, CH), CH),
        )

    def scatter_step(n, carry):
        @pl.when(n + 1 < N)
        def _():
            load_chunk(n + 1)

        @pl.when(n < N)
        def _():
            b = 2 * (n % 2)
            wait(wbuf.at[b], s_w.at[b])
            wait(wbuf.at[b + 1], s_w.at[b + 1])
            part = jnp.concatenate([dot_nt(grad[...], wbuf[b]), dot_nt(grad[...], wbuf[b + 1])], axis=1)
            m1o[n, 0] = part[256:320].astype(BF16)
            m1o[n, 1] = part[320:384].astype(BF16)
            send(m1o.at[n, 0], m1i.at[n, 0], s_send.at[10], s_m1.at[0, n], yp)
            send(m1o.at[n, 1], m1i.at[n, 1], s_send.at[11], s_m1.at[1, n], ym)
            pre[pend(n, 0)] = part[128:192]
            m2o[n, 0, 64:128] = part[192:256].astype(BF16)
            m2o[n, 1, 0:64] = part[384:448].astype(BF16)
            pre[pend(n, 1)] = part[448:512]
            pre[kept(n)] = part[0:128]

        @pl.when(jnp.logical_and(n >= 2, n < N + 2))
        def _():
            q = n - 2
            wait(m1i.at[0, 0], s_m1.at[0, q])
            m2o[q, 0, 0:64] = (pre[pend(q, 0)] + m1i[q, 0].astype(F32)).astype(BF16)
            send(m2o.at[q, 0], m2i.at[q, 0], s_send.at[12], s_m2.at[0, q], yp)
            wait(m1i.at[0, 0], s_m1.at[1, q])
            m2o[q, 1, 64:128] = (pre[pend(q, 1)] + m1i[q, 1].astype(F32)).astype(BF16)
            send(m2o.at[q, 1], m2i.at[q, 1], s_send.at[13], s_m2.at[1, q], ym)

        @pl.when(n >= 5)
        def _():
            q = n - 5
            wait(m2i.at[0, 0], s_m2.at[0, q])
            wait(m2i.at[0, 0], s_m2.at[1, q])
            cols = chunk(q)
            total = pre[kept(q)] + m2i[q, 0].astype(F32) + m2i[q, 1].astype(F32)
            e = total * gain_ref[:, cols]
            normed = (tok_ref[:, cols].astype(F32) - stat[0, :, 0:1]) * stat[1, :, 0:1]
            pre[kept(q)] = e
            pltpu.make_async_copy(pre.at[kept(q)], scaled_out.at[:, cols], s_out).start()
            stat[3] += jnp.broadcast_to(jnp.sum(e, axis=-1, keepdims=True), (128, 128))
            stat[4] += jnp.broadcast_to(jnp.sum(e * normed, axis=-1, keepdims=True), (128, 128))

        @pl.when(jnp.logical_and(n == STEP_REST, jnp.logical_not(early)))
        def _():
            image_gradient()

        return carry

    stat[3] = jnp.zeros((128, 128), F32)
    stat[4] = jnp.zeros((128, 128), F32)
    lax.fori_loop(0, N + 5, scatter_step, 0)

    own_image = t // 2
    for h in range(2):
        row_out[:, h * HALF:(h + 1) * HALF] = cotf[pl.ds(h * 8 + own_image, 1), :]
    lane = lax.broadcasted_iota(jnp.int32, (128, 128), 1)
    means = jnp.where(lane == 2, stat[3], stat[4]) * (1.0 / D)
    stat_out[...] = jnp.where(lane == 0, stat[0], jnp.where(lane == 1, stat[1], means))
    wait(scaled_out, s_out)

    wait(tx.at[0], s_small.at[0])
    wait(stack.at[pl.ds(0, 3)], s_small.at[2])
    wait(text.at[pl.ds(0, 48), pl.ds(0, HALF)], s_small.at[4])
    wait(text.at[pl.ds(0, 192), pl.ds(0, HALF)], s_small.at[15])
    wait(text.at[:, pl.ds(0, HALF)], s_small.at[6])
    wait(fold_in, s_small.at[8])

    @pl.when(early)
    def _():
        for _i in range(3):
            wait(cot, s_small.at[10])

    @pl.when(urgent)
    def _():
        for _i in range(3):
            wait(cot, s_small.at[17])

    for j in range(3):
        wait(hid.at[0], s_small.at[12 + j])
    for j in range(2):
        wait(ln.at[:, pl.ds(0, 128)], s_send.at[j])
        wait(w1.at[pl.ds(0, D // 4)], s_send.at[2 + j])
        wait(ln.at[:, pl.ds(0, 64)], s_send.at[5 + j])
        wait(w1.at[pl.ds(0, D // 4)], s_send.at[7 + j])
        wait(m1o.at[:, 0], s_send.at[10 + j])
        wait(m2o.at[:, 0], s_send.at[12 + j])
    wait(w1, s_send.at[4])
    wait(w1, s_send.at[9])


def finish_kernel(scaled_ref, tok_ref, stat_ref, row_ref, img_ref, img_out, tok_out):
    inverse = stat_ref[:, 1:2]
    normed = (tok_ref[...].astype(F32) - stat_ref[:, 0:1]) * inverse
    tok_out[...] = row_ref[...] + inverse * (scaled_ref[...] - stat_ref[:, 2:3] - normed * stat_ref[:, 3:4])
    img_out[...] = img_ref[...]


def body(
    picture_embeds, caption_embeds, picture_match_ids, caption_match_ids, logit_multiplier, logit_offset,
    branch_entries, rescale_factor, entry_projection_matrix, exit_projection_matrix,
):
    vmem = pl.BlockSpec(memory_space=pltpu.VMEM)
    smem = pl.BlockSpec(memory_space=pltpu.SMEM)
    anyw = pl.BlockSpec(memory_space=pl.ANY)
    dma = pltpu.SemaphoreType.DMA
    image_grad, scaled, stats, cot_row, _ = pl.pallas_call(
        kernel,
        out_shape=(
            jax.ShapeDtypeStruct((8, D), F32),
            jax.ShapeDtypeStruct((ROWS, D), F32),
            jax.ShapeDtypeStruct((ROWS, 128), F32),
            jax.ShapeDtypeStruct((1, D), F32),
            jax.ShapeDtypeStruct((3, D, HB), BF16),
        ),
        in_specs=[vmem, vmem, vmem, vmem, smem, smem, vmem, vmem, anyw, anyw],
        out_specs=(vmem, anyw, vmem, vmem, anyw),
        scratch_shapes=[
            pltpu.VMEM((G, 4 * ROWS, GC), BF16),
            pltpu.VMEM((4, GC, 4 * HB), BF16),
            pltpu.VMEM((4 * ROWS, 4 * HB), F32),
            pltpu.VMEM((4 * ROWS, 4 * HB), BF16),
            pltpu.VMEM((N, 2, 64, CH), BF16),
            pltpu.VMEM((N, 2, 128, CH), BF16),
            pltpu.VMEM((N, 2, 64, CH), BF16),
            pltpu.VMEM((N, 2, 128, CH), BF16),
            pltpu.VMEM((256, D), BF16),
            pltpu.VMEM((HB, D), BF16),
            pltpu.VMEM((4, 16, HALF), BF16),
            pltpu.VMEM((32, D), BF16),
            pltpu.VMEM((4, 8, D), F32),
            pltpu.VMEM((3, 8, D), F32),
            pltpu.VMEM((2, 8, D), F32),
            pltpu.VMEM((8, D), F32),
            pltpu.VMEM((16, HALF), BF16),
            pltpu.VMEM((16, HALF), F32),
            pltpu.VMEM((4, 8, HB), F32),
            pltpu.VMEM((5, 128, 128), F32),
            dma((14,)),
            dma((2, G)),
            dma((2, G)),
            dma((2, G)),
            dma((2, G)),
            dma((G,)),
            dma((G,)),
            dma((2, N)),
            dma((2, N)),
            dma((18,)),
            dma((3,)),
            dma((4,)),
            dma(()),
            dma(()),
        ],
        compiler_params=pltpu.CompilerParams(
            collective_id=0, has_side_effects=True, vmem_limit_bytes=62 * 2**20
        ),
    )(
        picture_embeds, caption_embeds, picture_match_ids.reshape(8, 128), caption_match_ids.reshape(8, 128),
        logit_multiplier, logit_offset, branch_entries, rescale_factor.reshape(1, D), entry_projection_matrix, exit_projection_matrix,
    )
    rows = 32

    def block(columns):
        return pl.BlockSpec((rows, columns), lambda i: (i, 0))

    def whole(count):
        return pl.BlockSpec((count, D), lambda i: (0, 0))

    return pl.pallas_call(
        finish_kernel,
        out_shape=(jax.ShapeDtypeStruct((8, D), F32), jax.ShapeDtypeStruct((ROWS, D), F32)),
        grid=(ROWS // rows,),
        in_specs=[block(D), block(D), block(128), whole(1), whole(8)],
        out_specs=(whole(8), block(D)),
        compiler_params=pltpu.CompilerParams(vmem_limit_bytes=62 * 2**20),
    )(scaled, branch_entries, stats, cot_row, image_grad)


def solution(mesh):
    in_specs = (
        P(("dp", "tensor"), None),
        P(("dp", "tensor"), None),
        P(),
        P(),
        P(),
        P(),
        P(("dp", "tensor"), None),
        P(),
        P(None, "tensor"),
        P("tensor", None),
    )
    out_specs = (P(("dp", "tensor"), None), P(("dp", "tensor"), None))
    return jax.shard_map(body, mesh=mesh, in_specs=in_specs, out_specs=out_specs, check_vma=False)
```

```python
import jax
import jax.numpy as jnp
from jax import lax
from jax.experimental import pallas as pl
from jax.experimental.pallas import tpu as pltpu
from jax.sharding import PartitionSpec as P

EPS = 1e-06
MESH = pl.DeviceIdType.MESH
F32 = jnp.float32
BF16 = jnp.bfloat16
D = 6144
HALF = D // 2
HB = 768
ROWS = 128
CH = 512
N = D // CH
GC = 256
G = D // GC
AHEAD = 6
LAG_FWD = 3
LAG_LOAD = 5
STEP_RELAY, STEP_TEXT, STEP_LOSS, STEP_IMAGE, STEP_COT, STEP_HIDDEN = 4, 10, 12, 17, 20, 24
AHEAD_FIRST = 4
STEP_REST = 3


def gelu_slope(values):
    cumulative = 0.5 * (1.0 + lax.erf(values * 0.7071067811865476))
    density = jnp.exp(-0.5 * values * values) * 0.3989422804014327
    return cumulative + values * density


def dot_nt(left, right):
    return lax.dot_general(left, right, (((1,), (1,)), ((), ())), preferred_element_type=F32)


def kernel(
    pic_ref, cap_ref, pic_ids, cap_ids, mult_ref, offs_ref, tok_ref, gain_ref, w1, wx_hbm,
    img_out, scaled_out, stat_out, row_out, w3,
    ln, wbuf, pre, grad, m1o, m2o, m1i, m2i, text, wx, stack, unit, fold, fold_in, tx, exact, cot, cotf, hid, stat,
    s_send, s_tok, s_fwd, s_z, s_x, s_own, s_for, s_m1, s_m2, s_small, s_hid, s_w, s_wx, s_out,
):
    d = lax.axis_index("dp")
    t = lax.axis_index("tensor")
    x, zh = d % 4, d // 4
    y, zl, c = t // 4, (t // 2) % 2, t % 2
    z = 2 * zh + zl

    def dev(x_, y_, z_, c_):
        return ((z_ // 2) * 4 + x_, y_ * 4 + (z_ % 2) * 2 + c_)

    yp, ym = dev(x, (y + 1) % 4, z, c), dev(x, (y + 3) % 4, z, c)
    zp, zm = dev(x, y, (z + 1) % 4, c), dev(x, y, (z + 3) % 4, c)
    xp, xm = dev((x + 1) % 4, y, z, c), dev((x + 3) % 4, y, z, c)
    mate = (d, y * 4 + zl * 2 + (1 - c))

    def send(src, dst, ssem, rsem, device):
        pltpu.make_async_remote_copy(
            src_ref=src, dst_ref=dst, send_sem=ssem, recv_sem=rsem, device_id=device, device_id_type=MESH
        ).start()

    def wait(ref, sem):
        pltpu.make_async_copy(ref, ref, sem).wait()

    near = (d, y * 4 + (1 - zl) * 2 + c)
    near_mate = (d, y * 4 + (1 - zl) * 2 + (1 - c))
    urgent = jnp.logical_and(zl == 0, c == 0)
    early = t == 0

    bar = pltpu.get_barrier_semaphore()

    def greet(r, _):
        for peer in (dev((x + r) % 4, y, z, c), dev(x, (y + r) % 4, z, c), dev(x, y, (z + r) % 4, c)):
            pl.semaphore_signal(bar, 1, device_id=peer, device_id_type=MESH)
        return 0

    lax.fori_loop(1, 4, greet, 0)
    for peer in (mate, near_mate):
        pl.semaphore_signal(bar, 1, device_id=peer, device_id_type=MESH)

    a0, b0 = jnp.where(c == 0, x, z), jnp.where(c == 0, z, x)

    def text_device(a, b):
        return dev(jnp.where(c == 0, a, b), y, jnp.where(c == 0, b, a), c)

    def text_rows(a, b):
        x_, z_ = jnp.where(c == 0, a, b), jnp.where(c == 0, b, a)
        return pl.ds(pl.multiple_of((((z_ // 2) * 4 + x_) * 2 + z_ % 2) * 16, 16), 16)

    text_cols = pl.ds(pl.multiple_of(c * HALF, HALF), HALF)

    pltpu.make_async_copy(wx_hbm, wx, s_wx).start()

    img = pic_ref[...].astype(F32)
    img_scale = lax.rsqrt(jnp.sum(img * img, axis=-1, keepdims=True) + EPS)
    img_exact = img * img_scale
    exact[...] = img_exact
    stat[2, 0:8] = jnp.broadcast_to(img_scale, (8, 128))
    stack[y] = jnp.concatenate([img_exact[:, :HALF], img_exact[:, HALF:]], axis=0).astype(BF16)
    cap = cap_ref[...].astype(F32)
    tx[c] = cap * lax.rsqrt(jnp.sum(cap * cap, axis=-1, keepdims=True) + EPS)

    def norm_rows(i, _):
        rows = pl.ds(pl.multiple_of(i * 16, 16), 16)
        values = tok_ref[rows, :].astype(F32)
        mean = jnp.mean(values, axis=-1, keepdims=True)
        centered = values - mean
        inverse = lax.rsqrt(jnp.mean(centered * centered, axis=-1, keepdims=True) + EPS)
        stat[0, rows] = jnp.broadcast_to(mean, (16, 128))
        stat[1, rows] = jnp.broadcast_to(inverse, (16, 128))
        out = (centered * inverse * gain_ref[...]).astype(BF16)
        for k in range(G):
            ln[k, rows, :] = out[:, k * GC:(k + 1) * GC]
        return 0

    lax.fori_loop(0, ROWS // 16, norm_rows, 0)

    pl.semaphore_wait(bar, 11)

    send(tx.at[c], tx.at[c], s_small.at[0], s_small.at[1], mate)

    xpar = x % 2

    def piece(k, par, p):
        return pl.ds(pl.multiple_of(k * GC + par * (GC // 2) + p * (GC // 4), GC // 4), GC // 4)

    def chunk(k):
        return pl.ds(pl.multiple_of(k * CH, CH), CH)

    def part_of(k):
        return pl.ds(pl.multiple_of(k * GC, GC), GC)

    def send_tokens(k):
        send(ln.at[k, pl.ds(0, 128)], ln.at[k, pl.ds(384, 128)], s_send.at[0], s_tok.at[0, k], yp)
        send(ln.at[k, pl.ds(0, 128)], ln.at[k, pl.ds(128, 128)], s_send.at[1], s_tok.at[1, k], ym)

    def send_weights(k):
        @pl.when(k < G - 1)
        def _():
            send(w1.at[piece(k, xpar, 0)], w3.at[1, piece(k, xpar, 0)], s_send.at[2], s_z.at[0, k], zm)
            send(w1.at[piece(k, xpar, 1)], w3.at[1, piece(k, xpar, 1)], s_send.at[3], s_z.at[1, k], zp)

        @pl.when(k == G - 1)
        def _():
            low, high = pl.ds(D - GC, GC // 2), pl.ds(D - GC // 2, GC // 2)
            send(w1.at[low], w3.at[1, low], s_send.at[2], s_z.at[0, k], zm)
            send(w1.at[high], w3.at[1, high], s_send.at[3], s_z.at[1, k], zp)

        send(w1.at[part_of(k)], w3.at[0, part_of(k)], s_send.at[4], s_own.at[k], mate)

    def first_weights(k, _):
        send_weights(k)
        return 0

    lax.fori_loop(0, AHEAD_FIRST, first_weights, 0)

    def first_tokens(k, _):
        send_tokens(k)
        return 0

    lax.fori_loop(0, AHEAD, first_tokens, 0)

    def send_images(r, _):
        send(stack.at[y], stack.at[y], s_small.at[2], s_small.at[3], dev(x, (y + r) % 4, z, c))
        return 0

    lax.fori_loop(1, 4, send_images, 0)

    wait(tx.at[0], s_small.at[1])
    both = jnp.concatenate([tx[0], tx[1]], axis=0)
    mine = jnp.where(c == 0, both[:, :HALF], both[:, HALF:]).astype(BF16)
    own_rows = text_rows(a0, b0)
    text[own_rows, text_cols] = mine

    def send_texts(i, _):
        part = text.at[own_rows, text_cols]
        send(part, part, s_small.at[4], s_small.at[5], text_device((a0 + i) % 4, b0))
        return 0

    lax.fori_loop(1, 4, send_texts, 0)

    def second(k, _):
        send_weights(k)
        return 0

    lax.fori_loop(AHEAD_FIRST, AHEAD, second, 0)
    pre[...] = jnp.zeros_like(pre)

    def load(k, b):
        pltpu.make_async_copy(w1.at[part_of(k)], wbuf.at[b, :, pl.ds(0, HB)], s_w.at[b]).start()
        for j in range(3):
            pltpu.make_async_copy(w3.at[j, part_of(k)], wbuf.at[b, :, pl.ds((j + 1) * HB, HB)], s_w.at[b]).start()

    def load_chunk(n):
        for h in range(2):
            load(2 * n + h, 2 * (n % 2) + h)

    def ids_of_images():
        row = pltpu.roll(pic_ids[pl.ds(d, 1), :], (128 - (t % 4) * 8) % 128, 1)
        image = lax.broadcasted_iota(jnp.int32, (32, 128), 0)
        lane = lax.broadcasted_iota(jnp.int32, (32, 128), 1)
        pick = lane == (image // 8) * 32 + image % 8
        values = jnp.broadcast_to(row.astype(F32), (32, 128))
        return jnp.sum(jnp.where(pick, values, 0.0), axis=-1, keepdims=True)

    def ids_of_texts():
        lane = lax.broadcasted_iota(jnp.int32, (1, 128), 1)
        halves = []
        for h in range(2):
            out = jnp.zeros((1, 128), F32)
            for i in range(4):
                row = cap_ids[h * 4 + i:h * 4 + i + 1, :]
                row = pltpu.roll(row, (i * 32 + 128 - y * 32) % 128, 1).astype(F32)
                out = jnp.where(lane // 32 == i, row, out)
            halves.append(out)
        return jnp.concatenate(halves, axis=1)

    def send_sums(r, _):
        other = (y + r) % 4
        send(fold.at[other], fold_in.at[r - 1], s_small.at[8], s_small.at[9], dev(x, other, z, c))
        return 0

    def send_rest(r, _):
        @pl.when(jnp.logical_not(jnp.logical_and(urgent, (y + r) % 4 == 0)))
        def _():
            send_sums(r, 0)

        return 0

    def image_gradient():
        wait(fold_in, s_small.at[9])
        total = fold[y] + fold_in[0] + fold_in[1] + fold_in[2]
        ex = exact[...]
        scale = stat[2, 0:8, 0:1]
        g = scale * (total - ex * jnp.sum(ex * total, axis=-1, keepdims=True))
        img_out[...] = g
        return g

    def gather_step(k, _):
        @pl.when(k < G)
        def _():
            wait(ln.at[0, pl.ds(0, 128)], s_tok.at[0, k])
            wait(ln.at[0, pl.ds(0, 128)], s_tok.at[1, k])
            send(ln.at[k, pl.ds(384, 64)], ln.at[k, pl.ds(256, 64)], s_send.at[5], s_fwd.at[0, k], yp)
            send(ln.at[k, pl.ds(192, 64)], ln.at[k, pl.ds(320, 64)], s_send.at[6], s_fwd.at[1, k], ym)

        @pl.when(k < G - 1)
        def _():
            wait(w3.at[1, pl.ds(0, GC // 4)], s_z.at[0, k])
            wait(w3.at[1, pl.ds(0, GC // 4)], s_z.at[1, k])
            send(w3.at[1, piece(k, xpar, 0)], w3.at[1, piece(k, xpar, 0)], s_send.at[7], s_x.at[0, k], xm)
            send(w3.at[1, piece(k, xpar, 1)], w3.at[1, piece(k, xpar, 1)], s_send.at[8], s_x.at[1, k], xp)

        @pl.when(k + AHEAD < G)
        def _():
            send_tokens(k + AHEAD)
            send_weights(k + AHEAD)

        @pl.when(jnp.logical_and(k >= LAG_FWD, k < G + LAG_FWD))
        def _():
            q = k - LAG_FWD
            wait(ln.at[0, pl.ds(0, 64)], s_fwd.at[0, q])
            wait(ln.at[0, pl.ds(0, 64)], s_fwd.at[1, q])

            @pl.when(q < G - 1)
            def _():
                wait(w3.at[1, pl.ds(0, GC // 4)], s_x.at[0, q])
                wait(w3.at[1, pl.ds(0, GC // 4)], s_x.at[1, q])

            @pl.when(q == G - 1)
            def _():
                wait(w3.at[1, pl.ds(0, GC // 2)], s_z.at[0, q])
                wait(w3.at[1, pl.ds(0, GC // 2)], s_z.at[1, q])

            send(w3.at[1, part_of(q)], w3.at[2, part_of(q)], s_send.at[9], s_for.at[q], mate)

        @pl.when(jnp.logical_and(k >= LAG_LOAD, k < G + LAG_LOAD))
        def _():
            q = k - LAG_LOAD
            wait(w3.at[0, pl.ds(0, GC)], s_own.at[q])
            wait(w3.at[2, pl.ds(0, GC)], s_for.at[q])
            load(q, q % 4)

        @pl.when(k >= LAG_LOAD + 1)
        def _():
            q = k - LAG_LOAD - 1
            b = q % 4
            wait(wbuf.at[b], s_w.at[b])

            def columns(j, _):
                cols = pl.ds(pl.multiple_of(j * HB, HB), HB)
                pre[:, cols] += jnp.dot(ln[q], wbuf[b, :, cols], preferred_element_type=F32)
                return 0

            lax.fori_loop(0, 4, columns, 0)

        @pl.when(k == G)
        def _():
            lax.fori_loop(1, 4, send_rest, 0)

        @pl.when(k == STEP_RELAY)
        def _():
            wait(text.at[pl.ds(0, 48), pl.ds(0, HALF)], s_small.at[5])

            def relay(i, _):
                part = text.at[text_rows((a0 + i // 3) % 4, b0), text_cols]
                send(part, part, s_small.at[15], s_small.at[16], text_device(a0, (b0 + 1 + i % 3) % 4))
                return 0

            lax.fori_loop(0, 12, relay, 0)

        @pl.when(k == STEP_TEXT)
        def _():
            wait(text.at[pl.ds(0, 192), pl.ds(0, HALF)], s_small.at[16])
            half = text.at[:, text_cols]
            send(half, half, s_small.at[6], s_small.at[7], mate)

        @pl.when(k == STEP_LOSS)
        def _():
            wait(stack.at[pl.ds(0, 3)], s_small.at[3])
            wait(text.at[:, pl.ds(0, HALF)], s_small.at[7])
            for pair in range(2):
                a = stack[2 * pair].astype(F32)
                b = stack[2 * pair + 1].astype(F32)
                unit[pair * 16:(pair + 1) * 16, :HALF] = jnp.concatenate([a[:8], b[:8]], axis=0).astype(BF16)
                unit[pair * 16:(pair + 1) * 16, HALF:] = jnp.concatenate([a[8:], b[8:]], axis=0).astype(BF16)
            multiplier = mult_ref[0]
            logits = multiplier * dot_nt(unit[...], text[...]) + offs_ref[0]
            labels = jnp.where(ids_of_images() == ids_of_texts(), 1.0, -1.0).astype(F32)
            coef = (-labels * multiplier * jax.nn.sigmoid(-labels * logits)).astype(BF16)

            def fold_cols(j, _):
                cols = pl.ds(pl.multiple_of(j * 1024, 1024), 1024)
                part = jnp.dot(coef, text[:, cols], preferred_element_type=F32)
                for i in range(4):
                    fold[i, :, cols] = part[i * 8:(i + 1) * 8]
                return 0

            lax.fori_loop(0, 6, fold_cols, 0)

            @pl.when(jnp.logical_and(urgent, y != 0))
            def _():
                send_sums(4 - y, 0)

        @pl.when(jnp.logical_and(k == STEP_IMAGE, early))
        def _():
            g = image_gradient()
            cot[...] = jnp.concatenate([g[:, :HALF], g[:, HALF:]], axis=0).astype(BF16)

            def send_cot(r, _):
                send(cot, cot, s_small.at[10], s_small.at[11], dev(x, (y + r) % 4, z, c))
                return 0

            lax.fori_loop(1, 4, send_cot, 0)

        @pl.when(jnp.logical_and(k == STEP_COT, urgent))
        def _():
            @pl.when(y != 0)
            def _():
                wait(cot, s_small.at[11])

            for peer in (near, near_mate, mate):
                send(cot, cot, s_small.at[17], s_small.at[11], peer)

        @pl.when(k == STEP_HIDDEN)
        def _():
            @pl.when(jnp.logical_not(urgent))
            def _():
                wait(cot, s_small.at[11])

            cotf[...] = cot[...].astype(F32)
            wait(wx, s_wx)
            for j in range(3):
                low = dot_nt(cot[...], wx[j * 256:(j + 1) * 256, :HALF])
                high = dot_nt(cot[...], wx[j * 256:(j + 1) * 256, HALF:])
                hid[0, :, j * 256:(j + 1) * 256] = low[:8] + high[8:]
            send(hid.at[0], hid.at[1], s_small.at[12], s_hid.at[0], mate)
            send(hid.at[0], hid.at[2], s_small.at[13], s_hid.at[1], near)
            send(hid.at[0], hid.at[3], s_small.at[14], s_hid.at[2], near_mate)

        return 0

    lax.fori_loop(0, G + LAG_LOAD + 1, gather_step, 0)
    load_chunk(0)

    for j in range(3):
        wait(hid.at[0], s_hid.at[j])

    def slope_block(i, _):
        r, j = i // 4, i % 4
        rows = pl.ds(pl.multiple_of(r * ROWS, ROWS), ROWS)
        cols = pl.ds(pl.multiple_of(j * HB, HB), HB)
        image = ((y + r) % 4) * 2 + zl
        factor = hid[j, pl.ds(image, 1), :]
        grad[rows, cols] = (factor * gelu_slope(pre[rows, cols])).astype(BF16)
        return 0

    lax.fori_loop(0, 16, slope_block, 0)

    def pend(n, side):
        return (
            pl.ds(pl.multiple_of((n // 6) * 128 + side * 64, 64), 64),
            pl.ds(pl.multiple_of((n % 6) * CH, CH), CH),
        )

    def kept(n):
        return (
            pl.ds(pl.multiple_of(256 + (n // 6) * 128, 128), 128),
            pl.ds(pl.multiple_of((n % 6) * CH, CH), CH),
        )

    def scatter_step(n, carry):
        @pl.when(n + 1 < N)
        def _():
            load_chunk(n + 1)

        @pl.when(n < N)
        def _():
            b = 2 * (n % 2)
            wait(wbuf.at[b], s_w.at[b])
            wait(wbuf.at[b + 1], s_w.at[b + 1])
            part = jnp.concatenate([dot_nt(grad[...], wbuf[b]), dot_nt(grad[...], wbuf[b + 1])], axis=1)
            m1o[n, 0] = part[256:320].astype(BF16)
            m1o[n, 1] = part[320:384].astype(BF16)
            send(m1o.at[n, 0], m1i.at[n, 0], s_send.at[10], s_m1.at[0, n], yp)
            send(m1o.at[n, 1], m1i.at[n, 1], s_send.at[11], s_m1.at[1, n], ym)
            pre[pend(n, 0)] = part[128:192]
            m2o[n, 0, 64:128] = part[192:256].astype(BF16)
            m2o[n, 1, 0:64] = part[384:448].astype(BF16)
            pre[pend(n, 1)] = part[448:512]
            pre[kept(n)] = part[0:128]

        @pl.when(jnp.logical_and(n >= 2, n < N + 2))
        def _():
            q = n - 2
            wait(m1i.at[0, 0], s_m1.at[0, q])
            m2o[q, 0, 0:64] = (pre[pend(q, 0)] + m1i[q, 0].astype(F32)).astype(BF16)
            send(m2o.at[q, 0], m2i.at[q, 0], s_send.at[12], s_m2.at[0, q], yp)
            wait(m1i.at[0, 0], s_m1.at[1, q])
            m2o[q, 1, 64:128] = (pre[pend(q, 1)] + m1i[q, 1].astype(F32)).astype(BF16)
            send(m2o.at[q, 1], m2i.at[q, 1], s_send.at[13], s_m2.at[1, q], ym)

        @pl.when(n >= 5)
        def _():
            q = n - 5
            wait(m2i.at[0, 0], s_m2.at[0, q])
            wait(m2i.at[0, 0], s_m2.at[1, q])
            cols = chunk(q)
            total = pre[kept(q)] + m2i[q, 0].astype(F32) + m2i[q, 1].astype(F32)
            e = total * gain_ref[:, cols]
            normed = (tok_ref[:, cols].astype(F32) - stat[0, :, 0:1]) * stat[1, :, 0:1]
            pre[kept(q)] = e
            pltpu.make_async_copy(pre.at[kept(q)], scaled_out.at[:, cols], s_out).start()
            stat[3] += jnp.broadcast_to(jnp.sum(e, axis=-1, keepdims=True), (128, 128))
            stat[4] += jnp.broadcast_to(jnp.sum(e * normed, axis=-1, keepdims=True), (128, 128))

        @pl.when(jnp.logical_and(n == STEP_REST, jnp.logical_not(early)))
        def _():
            image_gradient()

        return carry

    stat[3] = jnp.zeros((128, 128), F32)
    stat[4] = jnp.zeros((128, 128), F32)
    lax.fori_loop(0, N + 5, scatter_step, 0)

    own_image = t // 2
    for h in range(2):
        row_out[:, h * HALF:(h + 1) * HALF] = cotf[pl.ds(h * 8 + own_image, 1), :]
    lane = lax.broadcasted_iota(jnp.int32, (128, 128), 1)
    means = jnp.where(lane == 2, stat[3], stat[4]) * (1.0 / D)
    stat_out[...] = jnp.where(lane == 0, stat[0], jnp.where(lane == 1, stat[1], means))
    wait(scaled_out, s_out)

    wait(tx.at[0], s_small.at[0])
    wait(stack.at[pl.ds(0, 3)], s_small.at[2])
    wait(text.at[pl.ds(0, 48), pl.ds(0, HALF)], s_small.at[4])
    wait(text.at[pl.ds(0, 192), pl.ds(0, HALF)], s_small.at[15])
    wait(text.at[:, pl.ds(0, HALF)], s_small.at[6])
    wait(fold_in, s_small.at[8])

    @pl.when(early)
    def _():
        for _i in range(3):
            wait(cot, s_small.at[10])

    @pl.when(urgent)
    def _():
        for _i in range(3):
            wait(cot, s_small.at[17])

    for j in range(3):
        wait(hid.at[0], s_small.at[12 + j])
    for j in range(2):
        wait(ln.at[:, pl.ds(0, 128)], s_send.at[j])
        wait(w1.at[pl.ds(0, D // 4 + GC // 4)], s_send.at[2 + j])
        wait(ln.at[:, pl.ds(0, 64)], s_send.at[5 + j])
        wait(w1.at[pl.ds(0, D // 4 - GC // 4)], s_send.at[7 + j])
        wait(m1o.at[:, 0], s_send.at[10 + j])
        wait(m2o.at[:, 0], s_send.at[12 + j])
    wait(w1, s_send.at[4])
    wait(w1, s_send.at[9])


def finish_kernel(scaled_ref, tok_ref, stat_ref, row_ref, img_ref, img_out, tok_out):
    inverse = stat_ref[:, 1:2]
    normed = (tok_ref[...].astype(F32) - stat_ref[:, 0:1]) * inverse
    tok_out[...] = row_ref[...] + inverse * (scaled_ref[...] - stat_ref[:, 2:3] - normed * stat_ref[:, 3:4])
    img_out[...] = img_ref[...]


def body(
    picture_embeds, caption_embeds, picture_match_ids, caption_match_ids, logit_multiplier, logit_offset,
    branch_entries, rescale_factor, entry_projection_matrix, exit_projection_matrix,
):
    vmem = pl.BlockSpec(memory_space=pltpu.VMEM)
    smem = pl.BlockSpec(memory_space=pltpu.SMEM)
    anyw = pl.BlockSpec(memory_space=pl.ANY)
    dma = pltpu.SemaphoreType.DMA
    image_grad, scaled, stats, cot_row, _ = pl.pallas_call(
        kernel,
        out_shape=(
            jax.ShapeDtypeStruct((8, D), F32),
            jax.ShapeDtypeStruct((ROWS, D), F32),
            jax.ShapeDtypeStruct((ROWS, 128), F32),
            jax.ShapeDtypeStruct((1, D), F32),
            jax.ShapeDtypeStruct((3, D, HB), BF16),
        ),
        in_specs=[vmem, vmem, vmem, vmem, smem, smem, vmem, vmem, anyw, anyw],
        out_specs=(vmem, anyw, vmem, vmem, anyw),
        scratch_shapes=[
            pltpu.VMEM((G, 4 * ROWS, GC), BF16),
            pltpu.VMEM((4, GC, 4 * HB), BF16),
            pltpu.VMEM((4 * ROWS, 4 * HB), F32),
            pltpu.VMEM((4 * ROWS, 4 * HB), BF16),
            pltpu.VMEM((N, 2, 64, CH), BF16),
            pltpu.VMEM((N, 2, 128, CH), BF16),
            pltpu.VMEM((N, 2, 64, CH), BF16),
            pltpu.VMEM((N, 2, 128, CH), BF16),
            pltpu.VMEM((256, D), BF16),
            pltpu.VMEM((HB, D), BF16),
            pltpu.VMEM((4, 16, HALF), BF16),
            pltpu.VMEM((32, D), BF16),
            pltpu.VMEM((4, 8, D), F32),
            pltpu.VMEM((3, 8, D), F32),
            pltpu.VMEM((2, 8, D), F32),
            pltpu.VMEM((8, D), F32),
            pltpu.VMEM((16, HALF), BF16),
            pltpu.VMEM((16, HALF), F32),
            pltpu.VMEM((4, 8, HB), F32),
            pltpu.VMEM((5, 128, 128), F32),
            dma((14,)),
            dma((2, G)),
            dma((2, G)),
            dma((2, G)),
            dma((2, G)),
            dma((G,)),
            dma((G,)),
            dma((2, N)),
            dma((2, N)),
            dma((18,)),
            dma((3,)),
            dma((4,)),
            dma(()),
            dma(()),
        ],
        compiler_params=pltpu.CompilerParams(
            collective_id=0, has_side_effects=True, vmem_limit_bytes=62 * 2**20
        ),
    )(
        picture_embeds, caption_embeds, picture_match_ids.reshape(8, 128), caption_match_ids.reshape(8, 128),
        logit_multiplier, logit_offset, branch_entries, rescale_factor.reshape(1, D), entry_projection_matrix, exit_projection_matrix,
    )
    rows = 64

    def block(columns):
        return pl.BlockSpec((rows, columns), lambda i: (i, 0))

    def whole(count):
        return pl.BlockSpec((count, D), lambda i: (0, 0))

    return pl.pallas_call(
        finish_kernel,
        out_shape=(jax.ShapeDtypeStruct((8, D), F32), jax.ShapeDtypeStruct((ROWS, D), F32)),
        grid=(ROWS // rows,),
        in_specs=[block(D), block(D), block(128), whole(1), whole(8)],
        out_specs=(whole(8), block(D)),
        compiler_params=pltpu.CompilerParams(vmem_limit_bytes=62 * 2**20),
    )(scaled, branch_entries, stats, cot_row, image_grad)


def solution(mesh):
    in_specs = (
        P(("dp", "tensor"), None),
        P(("dp", "tensor"), None),
        P(),
        P(),
        P(),
        P(),
        P(("dp", "tensor"), None),
        P(),
        P(None, "tensor"),
        P("tensor", None),
    )
    out_specs = (P(("dp", "tensor"), None), P(("dp", "tensor"), None))
    return jax.shard_map(body, mesh=mesh, in_specs=in_specs, out_specs=out_specs, check_vma=False)
```
